512 devices in a mesh: section: 4 (over x), row: 8 (over z_hi, core), col: 16 (over y, z_lo).
Axes of the slice: x: 4, y: 4, z: 16 (z_hi: 4, z_lo: 4; z = z_hi * 4 + z_lo), core: 2. Of those that a mesh axis runs over, the one named last changes fastest.
Arguments:
- pair: bfloat16 [256, 256, 128], P(('section', 'row'), 'col'), may hold values from -6 to 6
- labels: int32 [256, 256], P(('section', 'row'), 'col'), may hold values from 0 to 63
- residue_mask: int32 [256], replicated, may hold values 0 or 1
- norm_gain: float32 [128], replicated, may hold values from 0.25 to 1.75
- in_weight: bfloat16 [128, 512], replicated, may hold values from -0.5 to 0.5
- gate_weight: bfloat16 [128, 128], replicated, may hold values from -0.5 to 0.5
- hidden_gain: float32 [128], replicated, may hold values from 0.25 to 1.75
- out_weight: bfloat16 [128, 128], replicated, may hold values from -0.5 to 0.5
- bin_weight: bfloat16 [128, 64], replicated, may hold values from -0.8984375 to 0.8984375
Outputs:
- pair_grad: bfloat16 [256, 256, 128], P(('section', 'row'), 'col')
The draws below stay inside these ranges and needn't reach their ends.
All inputs are finite; a program needn't handle non-finite values.
Results may differ from the reference program's by a relative error of at most 0.014.
Values may be sent and summed in bfloat16 or wider, within the bound.
A program may use at most 64 MiB of HBM per device.

```python
import jax
import jax.numpy as jnp
from jax import lax

PAIR = 128
HIDDEN_SIZE = 128
BINS = 64
RESIDUES = 256


def plant(drawn, rng, least, high):
    longest = drawn.shape.index(max(drawn.shape))
    spots = []
    for shift in (0, 1):
        where = [jax.random.randint(jax.random.fold_in(rng, axis), (), 0, length) for axis, length in enumerate(drawn.shape)]
        where[longest] = (where[longest] + shift) % drawn.shape[longest]
        spots.append(tuple(where))
    return drawn.at[spots[0]].set(least).at[spots[1]].set(high)


def shard_levels(own_key, dims, cuts, smallest, top_value):
    def one(dim, shards_of):
        heights = jax.random.uniform(jax.random.fold_in(jax.random.fold_in(own_key, 6), dim), (shards_of,), jnp.float32, smallest / len(cuts), top_value / len(cuts))
        return jnp.repeat(jnp.exp(heights), dims[dim] // shards_of).reshape((-1,) + (1,) * (len(dims) - dim - 1))

    loudness = one(*cuts[0])
    for cut in cuts[1:]:
        loudness = loudness * one(*cut)
    return loudness


def bell_draw(stream_key, shape, deviation, bound, pieces=(), held_as=jnp.bfloat16):
    entries = jax.random.normal(stream_key, shape, jnp.float32) * deviation
    if len(pieces) > 0:
        entries = shard_levels(stream_key, shape, pieces, -0.22, 0.18) * entries
    return jnp.clip(entries, min=-bound, max=bound).astype(held_as)


def setup_inputs(seed: int = 0) -> dict:
    keys = jax.random.split(jax.random.key(seed), 10)
    pair = bell_draw(keys[0], (RESIDUES, RESIDUES, PAIR), 1.0, 6.0, ((0, 32), (1, 16)))
    labels = plant(jax.random.randint(keys[1], (RESIDUES, RESIDUES), 0, BINS), jax.random.fold_in(keys[1], 1), 0, BINS - 1).astype(jnp.int32)
    residue_mask = plant((jax.random.randint(keys[2], (RESIDUES,), 0, 8) < 7).astype(jnp.int32), jax.random.fold_in(keys[2], 1), 0, 1)
    norm_gain = jnp.clip(1.0 + 0.15 * jax.random.normal(keys[3], (PAIR,), jnp.float32), 0.25, 1.75)
    in_weight = bell_draw(keys[4], (PAIR, 4 * HIDDEN_SIZE), PAIR ** -0.5, 0.5)
    gate_weight = bell_draw(keys[5], (PAIR, PAIR), PAIR ** -0.5, 0.5)
    hidden_gain = jnp.clip(1.0 + 0.15 * jax.random.normal(keys[6], (HIDDEN_SIZE,), jnp.float32), 0.25, 1.75)
    out_weight = bell_draw(keys[7], (HIDDEN_SIZE, PAIR), HIDDEN_SIZE ** -0.5, 0.5)
    bin_weight = bell_draw(keys[8], (PAIR, BINS), 0.15, 0.8984375)
    return dict(pair=pair, labels=labels, residue_mask=residue_mask, norm_gain=norm_gain, in_weight=in_weight, gate_weight=gate_weight, hidden_gain=hidden_gain, out_weight=out_weight, bin_weight=bin_weight)


def norm_parts(values, gain):
    centre = values - lax.optimization_barrier(jnp.mean(values, axis=-1, keepdims=True))
    inverse = lax.rsqrt(lax.optimization_barrier(jnp.mean(centre * centre, axis=-1, keepdims=True)) + 1e-05)
    normed = centre * inverse
    return (normed, inverse, normed * gain)

def norm_back(upstream, normed, inverse, gain):
    scaled = upstream * gain
    return inverse * (scaled - lax.optimization_barrier(jnp.mean(scaled, axis=-1, keepdims=True)) - normed * lax.optimization_barrier(jnp.mean(scaled * normed, axis=-1, keepdims=True)))

def reference(pair, labels, residue_mask, norm_gain, in_weight, gate_weight, hidden_gain, out_weight, bin_weight):
    mask_float = residue_mask.astype(jnp.float32)
    pair_mask = (mask_float[:, None] * mask_float[None, :])[:, :, None]
    pair_float = pair.astype(jnp.float32)
    normed_in, inverse_in, scaled_in = norm_parts(pair_float, norm_gain)
    inputs = scaled_in.astype(jnp.bfloat16)
    projected = jnp.dot(inputs, in_weight, preferred_element_type=jnp.float32)
    gate_a, value_a, gate_b, value_b = jnp.split(projected, 4, axis=-1)
    sig_a = jax.nn.sigmoid(gate_a)
    sig_b = jax.nn.sigmoid(gate_b)
    left = (sig_a * value_a * pair_mask).astype(jnp.bfloat16)
    right = (sig_b * value_b * pair_mask).astype(jnp.bfloat16)
    left_float = left.astype(jnp.float32)
    right_float = right.astype(jnp.float32)
    triangle = jnp.einsum('ikh,jkh->ijh', left_float, right_float)
    normed_t, inverse_t, scaled_t = norm_parts(triangle, hidden_gain)
    update = jnp.dot(scaled_t.astype(jnp.bfloat16), out_weight, preferred_element_type=jnp.float32)
    gate_out = jax.nn.sigmoid(jnp.dot(inputs, gate_weight, preferred_element_type=jnp.float32))
    pair_out = (pair_float + gate_out * update).astype(jnp.bfloat16)
    logits = jnp.dot(pair_out, bin_weight, preferred_element_type=jnp.float32).astype(jnp.bfloat16)
    logits_float = logits.astype(jnp.float32)
    symmetric = logits_float + jnp.transpose(logits_float, (1, 0, 2))
    weights = jnp.exp(symmetric)
    probs = weights / lax.optimization_barrier(jnp.sum(weights, axis=-1, keepdims=True))
    onehot = (labels[:, :, None] == jnp.arange(bin_weight.shape[1], dtype=jnp.int32)).astype(jnp.float32)
    grad_bins = (pair_mask * (probs - onehot)).astype(jnp.bfloat16)
    grad_float = grad_bins.astype(jnp.float32)
    grad_sym = (grad_float + jnp.transpose(grad_float, (1, 0, 2))).astype(jnp.bfloat16)
    grad_out = jnp.dot(grad_sym, bin_weight.T, preferred_element_type=jnp.float32)
    grad_gate = (grad_out * update * gate_out * (1.0 - gate_out)).astype(jnp.bfloat16)
    grad_update = (grad_out * gate_out).astype(jnp.bfloat16)
    grad_scaled = jnp.dot(grad_update, out_weight.T, preferred_element_type=jnp.float32)
    grad_triangle = norm_back(grad_scaled, normed_t, inverse_t, hidden_gain).astype(jnp.bfloat16)
    grad_tri_float = grad_triangle.astype(jnp.float32)
    grad_left = jnp.einsum('ijh,jkh->ikh', grad_tri_float, right_float)
    grad_right = jnp.einsum('ijh,ikh->jkh', grad_tri_float, left_float)
    grad_proj = jnp.concatenate([grad_left * value_a * pair_mask * sig_a * (1.0 - sig_a), grad_left * sig_a * pair_mask, grad_right * value_b * pair_mask * sig_b * (1.0 - sig_b), grad_right * sig_b * pair_mask], axis=-1).astype(jnp.bfloat16)
    grad_inputs = jnp.dot(grad_proj, in_weight.T, preferred_element_type=jnp.float32) + jnp.dot(grad_gate, gate_weight.T, preferred_element_type=jnp.float32)
    return (grad_out + norm_back(grad_inputs, normed_in, inverse_in, norm_gain)).astype(jnp.bfloat16)
```

```python
import functools

import jax
import jax.numpy as jnp
from jax import lax
from jax.experimental import pallas as pl
from jax.experimental.pallas import tpu as pltpu
from jax.sharding import PartitionSpec as P

MESH = pl.DeviceIdType.MESH
F32 = jnp.float32
BF16 = jnp.bfloat16


def norm_parts(values, gain):
    centre = values - jnp.mean(values, axis=-1, keepdims=True)
    inverse = lax.rsqrt(jnp.mean(centre * centre, axis=-1, keepdims=True) + 1e-05)
    normed = centre * inverse
    return (normed, inverse, normed * gain)


def norm_back(upstream, normed, inverse, gain):
    scaled = upstream * gain
    return inverse * (
        scaled
        - jnp.mean(scaled, axis=-1, keepdims=True)
        - normed * jnp.mean(scaled * normed, axis=-1, keepdims=True)
    )


def dot_nt(a, b):
    return lax.dot_general(a, b, (((1,), (1,)), ((), ())), preferred_element_type=F32)


def kernel(
    side,
    pair_ref,
    labels_ref,
    mask_ref,
    norm_gain_ref,
    in_weight_ref,
    gate_weight_ref,
    hidden_gain_ref,
    out_weight_ref,
    bin_weight_ref,
    out_ref,
    left_own,
    right_own,
    left_all,
    right_all,
    acc,
    tri_part,
    tri_in,
    logit_out,
    logit_in,
    label_out,
    label_in,
    gtri,
    gtri_wide,
    gl_part,
    gr_part,
    gl_in,
    gr_in,
    gl_sum,
    gr_sum,
    gl_own,
    gr_own,
    saved,
    s_left1,
    s_right1,
    s_left2,
    s_right2,
    s_tri,
    s_logit,
    s_label,
    s_gtri,
    s_gl1,
    s_gr1,
    s_gl2,
    s_gr2,
    r_left1,
    r_right1,
    r_left2,
    r_right2,
    r_tri,
    r_logit,
    r_label,
    r_gtri,
    r_gl1,
    r_gr1,
    r_gl2,
    r_gr2,
):
    half = side // 2
    x = lax.axis_index("section")
    row = lax.axis_index("row")
    col = lax.axis_index("col")
    zh = row // 2
    core = row % 2
    y = col // side
    zl = col % side
    my_k_core = zl // half
    my_k_slot = zl % half
    diagonal = jnp.logical_and(x == y, zh == zl)

    def device(dx, dy, dzh, dzl, dcore):
        return (dx, dzh * 2 + dcore, dy * side + dzl)

    def send(src, dst, send_sem, recv_sem, target):
        return pltpu.make_async_remote_copy(
            src_ref=src,
            dst_ref=dst,
            send_sem=send_sem,
            recv_sem=recv_sem,
            device_id=target,
            device_id_type=MESH,
        )

    def push(src, dst, send_sem, recv_sem, target, is_self):
        @pl.when(is_self)
        def _():
            pltpu.make_async_copy(src, dst, recv_sem).start()

        @pl.when(jnp.logical_not(is_self))
        def _():
            send(src, dst, send_sem, recv_sem, target).start()

    def drain(src, dst, send_sem, recv_sem, target, is_self):
        @pl.when(jnp.logical_not(is_self))
        def _():
            send(src, dst, send_sem, recv_sem, target).wait_send()

    def arrived(ref, sem):
        pltpu.make_async_copy(ref, ref, sem).wait()

    barrier = pltpu.get_barrier_semaphore()

    def greet(target, is_self):
        @pl.when(jnp.logical_not(is_self))
        def _():
            pl.semaphore_signal(barrier, inc=1, device_id=target, device_id_type=MESH)

    never = x < 0
    for step in range(1, 2 * side):
        other = (zl * 2 + core + step) % (2 * side)
        greet(device(x, y, zh, other // 2, other % 2), never)
    for step in range(1, side):
        greet(device(x, (y + step) % side, zh, zl, core), never)
        greet(device((x + step) % side, y, zh, zl, core), never)
    on_own_path = jnp.logical_and(diagonal, core == my_k_core)
    for there in range(side):
        greet(
            device(y, x, there, zh, my_k_core), jnp.logical_and(on_own_path, there == zh)
        )
    for slot in range(half):
        for there in range(2):
            source = core * half + slot
            greet(
                device(y, x, zl, source, there),
                jnp.logical_and(diagonal, jnp.logical_and(source == zl, there == core)),
            )
    for there in range(2):
        greet(device(y, x, zl, zh, there), jnp.logical_and(diagonal, there == core))
    greetings = 2 * side - 1 + 2 * (side - 1) + 2 * side + 2
    awaited = greetings - 2 * on_own_path.astype(jnp.int32) - diagonal.astype(jnp.int32)

    pair_float = pair_ref[...].astype(F32).reshape(128, 128)
    normed_in, inverse_in, scaled_in = norm_parts(pair_float, norm_gain_ref[...])
    inputs = scaled_in.astype(BF16)
    place = lax.broadcasted_iota(jnp.int32, (128, 256), 0)
    lane = lax.broadcasted_iota(jnp.int32, (128, 256), 1)
    mask_float = mask_ref[...].astype(F32)
    first_row = (x * side + zh) * 16 + core * 8
    first_col = col * 16
    mask_i = jnp.sum(
        jnp.where(lane == first_row + place // 16, mask_float, 0.0), axis=1, keepdims=True
    )
    mask_j = jnp.sum(
        jnp.where(lane == first_col + place % 16, mask_float, 0.0), axis=1, keepdims=True
    )
    pair_mask = mask_i * mask_j
    projected = jnp.dot(inputs, in_weight_ref[...], preferred_element_type=F32)
    sig_a = jax.nn.sigmoid(projected[:, 0:128])
    value_a = projected[:, 128:256]
    sig_b = jax.nn.sigmoid(projected[:, 256:384])
    value_b = projected[:, 384:512]
    right_own[...] = (sig_b * value_b * pair_mask).astype(BF16).reshape(8, 16, 128)
    left_own[...] = (sig_a * value_a * pair_mask).astype(BF16).reshape(8, 16, 128)
    label_out[...] = labels_ref[...].astype(F32)
    pl.semaphore_wait(barrier, awaited)

    def first_right(there):
        return (
            right_own,
            right_all.at[y, my_k_slot, core],
            s_right1.at[there],
            r_right1.at[my_k_slot, core],
            device(y, x, there, zh, my_k_core),
            jnp.logical_and(on_own_path, there == zh),
        )

    def first_left(there):
        return (
            left_own,
            left_all.at[y, my_k_slot, core],
            s_left1.at[there],
            r_left1.at[my_k_slot, core],
            device(x, y, zh, there, my_k_core),
            jnp.logical_and(there == zl, core == my_k_core),
        )

    def labels_to(there):
        return (
            label_out,
            label_in.at[core],
            s_label.at[there],
            r_label.at[core],
            device(y, x, zl, zh, there),
            jnp.logical_and(diagonal, there == core),
        )

    for there in range(side):
        push(*first_right(there))
    for there in range(side):
        push(*first_left(there))
    for there in range(2):
        push(*labels_to(there))

    saved[0] = normed_in
    saved[1] = sig_a
    saved[2] = value_a
    saved[3] = sig_b
    saved[4] = value_b
    saved[5] = jax.nn.sigmoid(jnp.dot(inputs, gate_weight_ref[...], preferred_element_type=F32))
    saved[6] = jnp.broadcast_to(pair_mask, (128, 128))
    saved[7] = jnp.broadcast_to(inverse_in, (128, 128))

    def second_left(slot, step):
        return send(
            left_all.at[y, slot],
            left_all.at[y, slot],
            s_left2.at[slot, step - 1],
            r_left2.at[y, slot],
            device(x, (y + step) % side, zh, zl, core),
        )

    def second_right(slot, step):
        return send(
            right_all.at[x, slot],
            right_all.at[x, slot],
            s_right2.at[slot, step - 1],
            r_right2.at[x, slot],
            device((x + step) % side, y, zh, zl, core),
        )

    for slot in range(half):
        for there in range(2):
            arrived(left_all.at[y, slot, there], r_left1.at[slot, there])
        for step in range(1, side):
            second_left(slot, step).start()
        for there in range(2):
            arrived(right_all.at[x, slot, there], r_right1.at[slot, there])
        for step in range(1, side):
            second_right(slot, step).start()

    acc[...] = jnp.zeros_like(acc)

    def tri_blocks(block, who):
        def body(index, carry):
            i_half = index // 8
            i_low = (index // 4) % 2 * 4
            j_half = (index // 2) % 2
            j_low = index % 2 * 4
            base = index // 4 * 64 + index % 4 * 4
            sums = [[acc[base + a * 16 + b] for b in range(4)] for a in range(4)]
            for slot in range(half):
                lefts = [left_all[who, slot, i_half, i_low + a].astype(F32) for a in range(4)]
                rights = [right_all[who, slot, j_half, j_low + b].astype(F32) for b in range(4)]
                for a in range(4):
                    for b in range(4):
                        product = lefts[a] * rights[b]
                        sums[a][b] = sums[a][b] + (product[0:8] + product[8:16])
            for a in range(4):
                for b in range(4):
                    acc[base + a * 16 + b] = sums[a][b]
            return carry

        lax.fori_loop(block * 8, block * 8 + 8, body, 0)

    def fold(part):
        def body(index, carry):
            at = part * 128 + index * 8
            tri_part[part, pl.ds(index * 8, 8)] = jnp.sum(acc[pl.ds(at, 8)], axis=1)
            return carry

        lax.fori_loop(0, 16, body, 0)

    def tri_copy():
        return send(
            tri_part.at[1 - core],
            tri_in,
            s_tri.at[0],
            r_tri.at[0],
            device(x, y, zh, zl, 1 - core),
        )

    for step in range(side):
        who = (y + step) % side
        if step > 0:
            for slot in range(half):
                arrived(left_all.at[who, slot], r_left2.at[who, slot])

        @pl.when(who != x)
        def _():
            for slot in range(half):
                arrived(right_all.at[who, slot], r_right2.at[who, slot])

        tri_blocks(1 - core, who)
        if step == side - 1:
            fold(1 - core)
            tri_copy().start()
        tri_blocks(core, who)
    fold(core)
    arrived(tri_in, r_tri.at[0])
    triangle = tri_part[core] + tri_in[...]

    hidden_gain = hidden_gain_ref[...]
    normed_t, inverse_t, scaled_t = norm_parts(triangle, hidden_gain)
    update = jnp.dot(scaled_t.astype(BF16), out_weight_ref[...], preferred_element_type=F32)
    gate_out = saved[5]
    pair_out = (pair_ref[...].astype(F32).reshape(128, 128) + gate_out * update).astype(BF16)
    logits = jnp.dot(pair_out, bin_weight_ref[...], preferred_element_type=F32)
    logits = logits.astype(BF16).astype(F32)
    blocks = logits.reshape(8, 2, 8, 64)
    for there in range(2):
        logit_out[there] = blocks[:, there].reshape(64, 64).astype(BF16)

    def logits_to(there):
        return (
            logit_out.at[there],
            logit_in.at[core],
            s_logit.at[there],
            r_logit.at[core],
            device(y, x, zl, zh, there),
            jnp.logical_and(diagonal, there == core),
        )

    for there in range(2):
        push(*logits_to(there))

    for there in range(2):
        arrived(label_in.at[there], r_label.at[there])
    place16 = lax.broadcasted_iota(jnp.int32, (128, 16), 0)
    lane16 = lax.broadcasted_iota(jnp.int32, (128, 16), 1)
    place8 = lax.broadcasted_iota(jnp.int32, (128, 8), 0)
    lane8 = lax.broadcasted_iota(jnp.int32, (128, 8), 1)
    spread = jnp.dot(
        (lane8 == place8 // 16).astype(F32), label_out[...], preferred_element_type=F32
    )
    label = jnp.sum(jnp.where(lane16 == place16 % 16, spread, 0.0), axis=1, keepdims=True)
    spread = jnp.dot(
        (lane16 == place16 % 16).astype(F32),
        label_in[...].reshape(16, 16),
        preferred_element_type=F32,
    )
    label_mirror = jnp.sum(
        jnp.where(lane16 == core * 8 + place16 // 16, spread, 0.0), axis=1, keepdims=True
    )
    bins = lax.broadcasted_iota(jnp.int32, (128, 64), 1)
    onehot = (label.astype(jnp.int32) == bins).astype(F32)
    onehot_mirror = (label_mirror.astype(jnp.int32) == bins).astype(F32)
    at_row = lax.broadcasted_iota(jnp.int32, (128, 128), 0)
    at_lane = lax.broadcasted_iota(jnp.int32, (128, 128), 1)
    turn = at_lane == (at_row // 8) % 2 * 64 + at_row % 8 * 8 + at_row // 16
    turn = turn.astype(F32).astype(BF16)
    mask_wide = saved[6]
    pair_mask = mask_wide[:, 0:64]

    for there in range(2):
        arrived(logit_in.at[there], r_logit.at[there])
    mirrored = jnp.dot(turn, logit_in[...].reshape(128, 64), preferred_element_type=F32)
    weights = jnp.exp(logits + mirrored)
    probs = weights / jnp.sum(weights, axis=-1, keepdims=True)
    grad_bins = (pair_mask * (probs - onehot)).astype(BF16).astype(F32)
    grad_mirror = (pair_mask * (probs - onehot_mirror)).astype(BF16).astype(F32)
    grad_sym = (grad_bins + grad_mirror).astype(BF16)
    grad_out = dot_nt(grad_sym, bin_weight_ref[...])
    grad_update = (grad_out * gate_out).astype(BF16)
    grad_scaled = dot_nt(grad_update, out_weight_ref[...])
    grad_triangle = norm_back(grad_scaled, normed_t, inverse_t, hidden_gain)
    gtri[core] = grad_triangle.astype(BF16)

    def gtri_copy():
        return send(
            gtri.at[core],
            gtri.at[core],
            s_gtri.at[0],
            r_gtri.at[core],
            device(x, y, zh, zl, 1 - core),
        )

    gtri_copy().start()
    grad_gate = (grad_out * update * gate_out * (1.0 - gate_out)).astype(BF16)
    saved[8] = grad_out
    saved[9] = dot_nt(grad_gate, gate_weight_ref[...])

    def widen(part):
        def body(index, carry):
            rows = gtri[part, pl.ds(index * 16, 16)].astype(F32)
            for a in range(16):
                gtri_wide[part * 128 + index * 16 + a] = jnp.broadcast_to(
                    rows[a : a + 1], (8, 128)
                )
            return carry

        lax.fori_loop(0, 8, body, 0)

    widen(core)
    arrived(gtri.at[1 - core], r_gtri.at[1 - core])
    widen(1 - core)

    def partial(out, source, who, slot, across, along):
        def body(part, carry):
            low = [jnp.zeros((8, 128), F32) for _ in range(8)]
            high = [jnp.zeros((8, 128), F32) for _ in range(8)]
            for n in range(16):
                tile = source[who, slot, n // 8, n % 8].astype(F32)
                for a in range(8):
                    factor = gtri_wide[(part * 8 + a) * across + n * along]
                    low[a] = low[a] + factor * tile[0:8]
                    high[a] = high[a] + factor * tile[8:16]
            for a in range(8):
                out[who, slot, part, a] = jnp.concatenate([low[a], high[a]], axis=0).astype(BF16)
            return carry

        lax.fori_loop(0, 2, body, 0)

    def third_left(slot, step):
        who = (y + step) % side
        return send(
            gl_part.at[who, slot],
            gl_in.at[y, slot],
            s_gl1.at[slot, step - 1],
            r_gl1.at[y, slot],
            device(x, who, zh, zl, core),
        )

    def third_right(slot, step):
        who = (x + step) % side
        return send(
            gr_part.at[who, slot],
            gr_in.at[x, slot],
            s_gr1.at[slot, step - 1],
            r_gr1.at[x, slot],
            device(who, y, zh, zl, core),
        )

    def partial_step(index, carry):
        slot = index // (side - 1)
        step = index % (side - 1) + 1
        partial(gr_part, left_all, (x + step) % side, slot, 1, 16)
        third_right(slot, step).start()
        partial(gl_part, right_all, (y + step) % side, slot, 16, 1)
        third_left(slot, step).start()
        return carry

    lax.fori_loop(0, half * (side - 1), partial_step, 0)

    def own_step(slot, carry):
        partial(gr_part, left_all, x, slot, 1, 16)
        partial(gl_part, right_all, y, slot, 16, 1)
        return carry

    lax.fori_loop(0, half, own_step, 0)

    def fourth_left(slot, there):
        owner = core * half + slot
        return (
            gl_sum.at[slot, there],
            gl_own.at[zl],
            s_gl2.at[slot, there],
            r_gl2.at[zl],
            device(x, y, zh, owner, there),
            jnp.logical_and(owner == zl, there == core),
        )

    def fourth_right(slot, there):
        owner = core * half + slot
        return (
            gr_sum.at[slot, there],
            gr_own.at[zh],
            s_gr2.at[slot, there],
            r_gr2.at[zh],
            device(y, x, zl, owner, there),
            jnp.logical_and(diagonal, jnp.logical_and(owner == zl, there == core)),
        )

    def sum_leg(total, part, come, sems, me, slot):
        for step in range(1, side):
            who = (me + step) % side
            arrived(come.at[who, slot], sems.at[who, slot])
        for there in range(2):
            value = part[me, slot, there].astype(F32)
            for step in range(1, side):
                value = value + come[(me + step) % side, slot, there].astype(F32)
            total[slot, there] = value.astype(BF16)

    for slot in range(half):
        sum_leg(gr_sum, gr_part, gr_in, r_gr1, x, slot)
        for there in range(2):
            push(*fourth_right(slot, there))
        sum_leg(gl_sum, gl_part, gl_in, r_gl1, y, slot)
        for there in range(2):
            push(*fourth_left(slot, there))

    def total_of(own, sems):
        value = None
        for there in range(side):
            arrived(own.at[there], sems.at[there])
            term = own[there].astype(F32)
            value = term if value is None else value + term
        return value.reshape(128, 128)

    grad_left = total_of(gl_own, r_gl2)
    sig_a = saved[1]
    value_a = saved[2]
    masked = grad_left * mask_wide
    proj_0 = (masked * value_a * sig_a * (1.0 - sig_a)).astype(BF16)
    proj_1 = (masked * sig_a).astype(BF16)
    grad_right = total_of(gr_own, r_gr2)
    sig_b = saved[3]
    value_b = saved[4]
    masked = grad_right * mask_wide
    proj_2 = (masked * value_b * sig_b * (1.0 - sig_b)).astype(BF16)
    proj_3 = (masked * sig_b).astype(BF16)
    grad_proj = jnp.concatenate([proj_0, proj_1, proj_2, proj_3], axis=-1)
    grad_inputs = dot_nt(grad_proj, in_weight_ref[...]) + saved[9]
    result = saved[8] + norm_back(grad_inputs, saved[0], saved[7], norm_gain_ref[...])
    out_ref[...] = result.astype(BF16).reshape(8, 16, 128)

    for there in range(side):
        drain(*first_right(there))
        drain(*first_left(there))
    for there in range(2):
        drain(*labels_to(there))
        drain(*logits_to(there))
    tri_copy().wait_send()
    gtri_copy().wait_send()
    for slot in range(half):
        for step in range(1, side):
            second_left(slot, step).wait_send()
            second_right(slot, step).wait_send()
            third_left(slot, step).wait_send()
            third_right(slot, step).wait_send()
        for there in range(2):
            drain(*fourth_left(slot, there))
            drain(*fourth_right(slot, there))


def local(
    pair,
    labels,
    residue_mask,
    norm_gain,
    in_weight,
    gate_weight,
    hidden_gain,
    out_weight,
    bin_weight,
):
    side = lax.axis_size("section")
    half = side // 2
    tile = (8, 16, 128)
    sems = [
        (side,),
        (side,),
        (half, side - 1),
        (half, side - 1),
        (1,),
        (2,),
        (2,),
        (1,),
        (half, side - 1),
        (half, side - 1),
        (half, 2),
        (half, 2),
        (half, 2),
        (half, 2),
        (side, half),
        (side, half),
        (1,),
        (2,),
        (2,),
        (2,),
        (side, half),
        (side, half),
        (side,),
        (side,),
    ]
    gathered = pltpu.VMEM((side, half, 2) + tile, BF16)
    residues = residue_mask.shape[0]
    if residues < 256:
        residue_mask = jnp.pad(residue_mask, (0, 256 - residues))
    return pl.pallas_call(
        functools.partial(kernel, side),
        out_shape=jax.ShapeDtypeStruct(tile, BF16),
        in_specs=[pl.BlockSpec(memory_space=pltpu.VMEM)] * 9,
        out_specs=pl.BlockSpec(memory_space=pltpu.VMEM),
        scratch_shapes=[
            pltpu.VMEM(tile, BF16),
            pltpu.VMEM(tile, BF16),
            gathered,
            gathered,
            pltpu.VMEM((256, 8, 128), F32),
            pltpu.VMEM((2, 128, 128), F32),
            pltpu.VMEM((128, 128), F32),
            pltpu.VMEM((2, 64, 64), BF16),
            pltpu.VMEM((2, 64, 64), BF16),
            pltpu.VMEM((8, 16), F32),
            pltpu.VMEM((2, 8, 16), F32),
            pltpu.VMEM((2, 128, 128), BF16),
            pltpu.VMEM((256, 8, 128), F32),
            gathered,
            gathered,
            gathered,
            gathered,
            pltpu.VMEM((half, 2) + tile, BF16),
            pltpu.VMEM((half, 2) + tile, BF16),
            pltpu.VMEM((side,) + tile, BF16),
            pltpu.VMEM((side,) + tile, BF16),
            pltpu.VMEM((10, 128, 128), F32),
        ]
        + [pltpu.SemaphoreType.DMA(shape) for shape in sems],
        compiler_params=pltpu.CompilerParams(
            collective_id=0, has_side_effects=True, vmem_limit_bytes=32 * 1024 * 1024
        ),
    )(
        pair,
        labels,
        residue_mask[None, :],
        norm_gain[None, :],
        in_weight,
        gate_weight,
        hidden_gain[None, :],
        out_weight,
        bin_weight,
    )


def solution(mesh):
    placed = (
        P(("section", "row"), "col", None),
        P(("section", "row"), "col"),
        P(),
        P(),
        P(),
        P(),
        P(),
        P(),
        P(),
    )
    return jax.shard_map(
        local,
        mesh=mesh,
        in_specs=placed,
        out_specs=P(("section", "row"), "col", None),
        check_vma=False,
    )
```

```python
import functools

import jax
import jax.numpy as jnp
from jax import lax
from jax.experimental import pallas as pl
from jax.experimental.pallas import tpu as pltpu
from jax.sharding import PartitionSpec as P

MESH = pl.DeviceIdType.MESH
F32 = jnp.float32
BF16 = jnp.bfloat16


def norm_parts(values, gain):
    centre = values - jnp.mean(values, axis=-1, keepdims=True)
    inverse = lax.rsqrt(jnp.mean(centre * centre, axis=-1, keepdims=True) + 1e-05)
    normed = centre * inverse
    return (normed, inverse, normed * gain)


def norm_back(upstream, normed, inverse, gain):
    scaled = upstream * gain
    return inverse * (
        scaled
        - jnp.mean(scaled, axis=-1, keepdims=True)
        - normed * jnp.mean(scaled * normed, axis=-1, keepdims=True)
    )


def dot_nt(a, b):
    return lax.dot_general(a, b, (((1,), (1,)), ((), ())), preferred_element_type=F32)


def kernel(
    side,
    pair_hbm,
    labels_hbm,
    mask_hbm,
    norm_gain_hbm,
    in_weight_hbm,
    gate_weight_hbm,
    hidden_gain_hbm,
    out_weight_hbm,
    bin_weight_hbm,
    out_ref,
    pair_ref,
    labels_ref,
    mask_ref,
    norm_gain_ref,
    in_weight_ref,
    gate_weight_ref,
    hidden_gain_ref,
    out_weight_ref,
    bin_weight_ref,
    loaded,
    left_own,
    right_own,
    left_all,
    right_all,
    acc,
    tri_part,
    tri_in,
    logit_out,
    logit_in,
    label_out,
    label_in,
    left_x,
    gtri,
    gtri_float,
    gl_part,
    gl_in,
    gr_acc,
    gl_sum,
    gr_sum,
    gl_own,
    gr_own,
    saved,
    s_left1,
    s_right1,
    s_left2,
    s_right2,
    s_tri,
    s_logit,
    s_label,
    s_left_x,
    s_gtri,
    s_gl1,
    s_gl2,
    s_gr2,
    r_left1,
    r_right1,
    r_left2,
    r_right2,
    r_tri,
    r_logit,
    r_label,
    r_left_x,
    r_gtri,
    r_gl1,
    r_gl2,
    r_gr2,
):
    half = side // 2
    x = lax.axis_index("section")
    row = lax.axis_index("row")
    col = lax.axis_index("col")
    zh = row // 2
    core = row % 2
    y = col // side
    zl = col % side
    my_k_core = zl // half
    my_k_slot = zl % half
    diagonal = jnp.logical_and(x == y, zh == zl)

    def turned(a, b):
        return (2 * a + side // 2 - b + side) % side

    mine = turned(y, x)
    meet = turned(x, y)

    def device(dx, dy, dzh, dzl, dcore):
        return (dx, dzh * 2 + dcore, dy * side + dzl)

    def send(src, dst, send_sem, recv_sem, target):
        return pltpu.make_async_remote_copy(
            src_ref=src,
            dst_ref=dst,
            send_sem=send_sem,
            recv_sem=recv_sem,
            device_id=target,
            device_id_type=MESH,
        )

    def push(src, dst, send_sem, recv_sem, target, is_self):
        @pl.when(is_self)
        def _():
            pltpu.make_async_copy(src, dst, recv_sem).start()

        @pl.when(jnp.logical_not(is_self))
        def _():
            send(src, dst, send_sem, recv_sem, target).start()

    def drain(src, dst, send_sem, recv_sem, target, is_self):
        @pl.when(jnp.logical_not(is_self))
        def _():
            send(src, dst, send_sem, recv_sem, target).wait_send()

    def arrived(ref, sem):
        pltpu.make_async_copy(ref, ref, sem).wait()

    barrier = pltpu.get_barrier_semaphore()

    operands = (
        (pair_hbm, pair_ref),
        (norm_gain_hbm, norm_gain_ref),
        (in_weight_hbm, in_weight_ref),
        (mask_hbm, mask_ref),
        (labels_hbm, labels_ref),
        (gate_weight_hbm, gate_weight_ref),
        (hidden_gain_hbm, hidden_gain_ref),
        (out_weight_hbm, out_weight_ref),
        (bin_weight_hbm, bin_weight_ref),
    )

    def load(index):
        return pltpu.make_async_copy(*operands[index], loaded.at[index])

    def greet(target, is_self=None):
        def signal():
            pl.semaphore_signal(barrier, inc=1, device_id=target, device_id_type=MESH)

        if is_self is None:
            signal()
        else:
            pl.when(jnp.logical_not(is_self))(signal)

    on_own_path = jnp.logical_and(
        jnp.logical_and(x == y, meet == x), jnp.logical_and(zh == zl, core == my_k_core)
    )
    for there in range(side):
        greet(
            device(meet, x, there, zh, my_k_core), jnp.logical_and(on_own_path, there == zh)
        )
    for slot in range(half):
        for there in range(2):
            source = core * half + slot
            greet(
                device(y, mine, zl, source, there),
                jnp.logical_and(on_own_path, jnp.logical_and(source == zl, there == core)),
            )
    for index in range(9):
        load(index).start()
    for step in range(1, 2 * side):
        other = (zl * 2 + core + step) % (2 * side)
        greet(device(x, y, zh, other // 2, other % 2))
    for step in range(1, side):
        greet(device(x, (y + step) % side, zh, zl, core))
        greet(device((x + step) % side, y, zh, zl, core))
        greet(device((x + step) % side, y, zh, zl, 1 - core))
    greetings = 2 * side - 1 + 3 * (side - 1) + 2 * side
    awaited = greetings - 2 * on_own_path.astype(jnp.int32)

    for index in range(5):
        load(index).wait()
    pair_float = pair_ref[...].astype(F32).reshape(128, 128)
    normed_in, inverse_in, scaled_in = norm_parts(pair_float, norm_gain_ref[...])
    inputs = scaled_in.astype(BF16)
    place = lax.broadcasted_iota(jnp.int32, (128, 256), 0)
    lane = lax.broadcasted_iota(jnp.int32, (128, 256), 1)
    mask_float = mask_ref[...].astype(F32)
    first_row = (x * side + zh) * 16 + core * 8
    first_col = col * 16
    mask_i = jnp.sum(
        jnp.where(lane == first_row + place // 16, mask_float, 0.0), axis=1, keepdims=True
    )
    mask_j = jnp.sum(
        jnp.where(lane == first_col + place % 16, mask_float, 0.0), axis=1, keepdims=True
    )
    pair_mask = mask_i * mask_j
    projected = jnp.dot(inputs, in_weight_ref[...], preferred_element_type=F32)
    sig_a = jax.nn.sigmoid(projected[:, 0:128])
    value_a = projected[:, 128:256]
    sig_b = jax.nn.sigmoid(projected[:, 256:384])
    value_b = projected[:, 384:512]
    right_own[...] = (sig_b * value_b * pair_mask).astype(BF16).reshape(8, 16, 128)
    left_own[...] = (sig_a * value_a * pair_mask).astype(BF16).reshape(8, 16, 128)
    label_out[...] = labels_ref[...].astype(F32)
    pl.semaphore_wait(barrier, awaited)

    def first_right(there):
        return (
            right_own,
            right_all.at[y, my_k_slot, core],
            s_right1.at[there],
            r_right1.at[my_k_slot, core],
            device(meet, x, there, zh, my_k_core),
            jnp.logical_and(on_own_path, there == zh),
        )

    def first_left(there):
        return (
            left_own,
            left_all.at[y, my_k_slot, core],
            s_left1.at[there],
            r_left1.at[my_k_slot, core],
            device(x, y, zh, there, my_k_core),
            jnp.logical_and(there == zl, core == my_k_core),
        )

    def labels_to(there):
        return (
            label_out,
            label_in.at[core],
            s_label.at[there],
            r_label.at[core],
            device(y, x, zl, zh, there),
            jnp.logical_and(diagonal, there == core),
        )

    my_turn = my_k_slot * 2 + core
    for phase in range(side):
        push(*first_right((my_turn + phase) % side))
    for there in range(side):
        push(*first_left(there))

    for index in range(5, 9):
        load(index).wait()

    saved[0] = normed_in
    saved[1] = sig_a
    saved[2] = value_a
    saved[3] = sig_b
    saved[4] = value_b
    saved[5] = jax.nn.sigmoid(jnp.dot(inputs, gate_weight_ref[...], preferred_element_type=F32))
    saved[6] = jnp.broadcast_to(pair_mask, (128, 128))
    saved[7] = jnp.broadcast_to(inverse_in, (128, 128))

    def second_left(slot, step):
        return send(
            left_all.at[y, slot],
            left_all.at[y, slot],
            s_left2.at[slot, step - 1],
            r_left2.at[y, slot],
            device(x, (y + step) % side, zh, zl, core),
        )

    def turn_of(phase):
        index = (zh - phase + side) % side
        return index // 2, index % 2

    def second_right(slot, part, step):
        return send(
            right_all.at[mine, slot, part],
            right_all.at[mine, slot, part],
            s_right2.at[slot, part, step - 1],
            r_right2.at[mine, slot, part],
            device((x + step) % side, y, zh, zl, core),
        )

    for slot in range(half):
        for there in range(2):
            arrived(left_all.at[y, slot, there], r_left1.at[slot, there])
        for step in range(1, side):
            second_left(slot, step).start()

    def forward(phase):
        slot, part = turn_of(phase)
        arrived(right_all.at[mine, slot, part], r_right1.at[slot, part])
        for step in range(1, side):
            second_right(slot, part, step).start()

    acc[...] = jnp.zeros_like(acc)

    def tri_blocks(i_half, slot, j_half):
        def body(index, carry):
            i_low = index // 2 * 4
            j_low = index % 2 * 4
            base = (i_half * 8 + i_low) * 16 + j_half * 8 + j_low
            sums = [[acc[base + a * 16 + b] for b in range(4)] for a in range(4)]
            for who in range(side):
                lefts = [left_all[who, slot, i_half, i_low + a].astype(F32) for a in range(4)]
                rights = [right_all[who, slot, j_half, j_low + b].astype(F32) for b in range(4)]
                for a in range(4):
                    for b in range(4):
                        product = lefts[a] * rights[b]
                        sums[a][b] = sums[a][b] + (product[0:8] + product[8:16])
            for a in range(4):
                for b in range(4):
                    acc[base + a * 16 + b] = sums[a][b]
            return carry

        lax.fori_loop(0, 4, body, 0)

    def fold(part):
        def body(index, carry):
            at = part * 128 + index * 8
            tri_part[part, pl.ds(index * 8, 8)] = jnp.sum(acc[pl.ds(at, 8)], axis=1)
            return carry

        lax.fori_loop(0, 16, body, 0)

    def tri_copy():
        return send(
            tri_part.at[1 - core],
            tri_in,
            s_tri.at[0],
            r_tri.at[0],
            device(x, y, zh, zl, 1 - core),
        )

    forward(0)
    for phase in range(side):
        if phase < side - 1:
            forward(phase + 1)
        slot, part = turn_of(phase)
        if phase == 0:
            for step in range(1, side):
                for there in range(half):
                    who = (y + step) % side
                    arrived(left_all.at[who, there], r_left2.at[who, there])
        for step in range(1, side):
            who = (mine + step) % side
            arrived(right_all.at[who, slot, part], r_right2.at[who, slot, part])
        if phase == side - 1:
            for there in range(2):
                push(*labels_to(there))
        tri_blocks(1 - core, slot, part)
        if phase == side - 1:
            fold(1 - core)
            tri_copy().start()
        tri_blocks(core, slot, part)
    fold(core)
    arrived(tri_in, r_tri.at[0])
    triangle = tri_part[core] + tri_in[...]

    hidden_gain = hidden_gain_ref[...]
    normed_t, inverse_t, scaled_t = norm_parts(triangle, hidden_gain)
    update = jnp.dot(scaled_t.astype(BF16), out_weight_ref[...], preferred_element_type=F32)
    gate_out = saved[5]
    pair_out = (pair_ref[...].astype(F32).reshape(128, 128) + gate_out * update).astype(BF16)
    logits = dot_nt(pair_out, bin_weight_ref[...])
    logits = logits.astype(BF16).astype(F32)
    blocks = logits.reshape(8, 2, 8, 64)
    for there in range(2):
        logit_out[there] = blocks[:, there].reshape(64, 64).astype(BF16)

    def logits_to(there):
        return (
            logit_out.at[there],
            logit_in.at[core],
            s_logit.at[there],
            r_logit.at[core],
            device(y, x, zl, zh, there),
            jnp.logical_and(diagonal, there == core),
        )

    for there in range(2):
        push(*logits_to(there))

    def left_to(step):
        who = (x + step) % side
        return send(
            left_all.at[turned(y, who)],
            left_x.at[x],
            s_left_x.at[step - 1],
            r_left_x.at[x],
            device(who, y, zh, zl, core),
        )

    for step in range(1, side):
        left_to(step).start()
    pltpu.make_async_copy(left_all.at[mine], left_x.at[x], r_left_x.at[x]).start()

    for there in range(2):
        arrived(label_in.at[there], r_label.at[there])
    place16 = lax.broadcasted_iota(jnp.int32, (128, 16), 0)
    lane16 = lax.broadcasted_iota(jnp.int32, (128, 16), 1)
    place8 = lax.broadcasted_iota(jnp.int32, (128, 8), 0)
    lane8 = lax.broadcasted_iota(jnp.int32, (128, 8), 1)
    spread = jnp.dot(
        (lane8 == place8 // 16).astype(F32), label_out[...], preferred_element_type=F32
    )
    label = jnp.sum(jnp.where(lane16 == place16 % 16, spread, 0.0), axis=1, keepdims=True)
    spread = jnp.dot(
        (lane16 == place16 % 16).astype(F32),
        label_in[...].reshape(16, 16),
        preferred_element_type=F32,
    )
    label_mirror = jnp.sum(
        jnp.where(lane16 == core * 8 + place16 // 16, spread, 0.0), axis=1, keepdims=True
    )
    bins = lax.broadcasted_iota(jnp.int32, (128, 64), 1)
    onehot = (label.astype(jnp.int32) == bins).astype(F32)
    onehot_mirror = (label_mirror.astype(jnp.int32) == bins).astype(F32)
    at_row = lax.broadcasted_iota(jnp.int32, (128, 128), 0)
    at_lane = lax.broadcasted_iota(jnp.int32, (128, 128), 1)
    turn = at_lane == (at_row // 8) % 2 * 64 + at_row % 8 * 8 + at_row // 16
    turn = turn.astype(F32).astype(BF16)
    mask_wide = saved[6]
    pair_mask = mask_wide[:, 0:64]

    for there in range(2):
        arrived(logit_in.at[there], r_logit.at[there])
    mirrored = jnp.dot(turn, logit_in[...].reshape(128, 64), preferred_element_type=F32)
    weights = jnp.exp(logits + mirrored)
    probs = weights / jnp.sum(weights, axis=-1, keepdims=True)
    grad_bins = (pair_mask * (probs - onehot)).astype(BF16).astype(F32)
    grad_mirror = (pair_mask * (probs - onehot_mirror)).astype(BF16).astype(F32)
    grad_sym = (grad_bins + grad_mirror).astype(BF16)
    grad_out = jnp.dot(grad_sym, bin_weight_ref[...], preferred_element_type=F32)
    grad_update = (grad_out * gate_out).astype(BF16)
    grad_scaled = dot_nt(grad_update, out_weight_ref[...])
    grad_triangle = norm_back(grad_scaled, normed_t, inverse_t, hidden_gain)
    gtri[x, core] = grad_triangle.astype(BF16)

    def gtri_to(step):
        other = (x * 2 + core + step) % (2 * side)
        return send(
            gtri.at[x, core],
            gtri.at[x, core],
            s_gtri.at[step - 1],
            r_gtri.at[x, core],
            device(other // 2, y, zh, zl, other % 2),
        )

    for step in range(1, 2 * side):
        gtri_to(step).start()
    grad_gate = (grad_out * update * gate_out * (1.0 - gate_out)).astype(BF16)
    saved[8] = grad_out
    saved[9] = dot_nt(grad_gate, gate_weight_ref[...])

    def widen(who, part):
        gtri_float[who, part] = gtri[who, part].astype(F32)

    widen(x, core)
    arrived(gtri.at[x, 1 - core], r_gtri.at[x, 1 - core])
    widen(x, 1 - core)

    def products(sums, tile_of, factor_of):
        low, high = list(sums[0:8]), list(sums[8:16])
        for n in range(16):
            tile = tile_of(n).astype(F32)
            for a in range(8):
                factor = jnp.broadcast_to(factor_of(n, a), (8, 128))
                low[a] = low[a] + factor * tile[0:8]
                high[a] = high[a] + factor * tile[8:16]
        return low + high

    nothing = [jnp.zeros((8, 128), F32) for _ in range(16)]

    def partial_left(who, slot, part):
        sums = products(
            nothing,
            lambda n: right_all[who, slot, n // 8, n % 8],
            lambda n, a: gtri_float[x, part, pl.ds(a * 16 + n, 1)],
        )
        for a in range(8):
            gl_part[who, slot, part, a] = jnp.concatenate(
                [sums[a], sums[a + 8]], axis=0
            ).astype(BF16)

    def third_left(slot, part, step):
        who = (y + step) % side
        return send(
            gl_part.at[who, slot, part],
            gl_in.at[y, slot, part],
            s_gl1.at[slot, part, step - 1],
            r_gl1.at[y, slot, part],
            device(x, who, zh, zl, core),
        )

    def partials_left(phase):
        slot, part = turn_of(phase)

        def body(step, carry):
            partial_left((y + step) % side, slot, part)

            @pl.when(step < side)
            def _():
                third_left(slot, part, step).start()

            return carry

        lax.fori_loop(1, side + 1, body, 0)

    def fourth_left(slot, there):
        owner = core * half + slot
        return (
            gl_sum.at[slot, there],
            gl_own.at[zl],
            s_gl2.at[slot, there],
            r_gl2.at[zl],
            device(x, y, zh, owner, there),
            jnp.logical_and(owner == zl, there == core),
        )

    def fourth_right(slot, there):
        owner = core * half + slot
        return (
            gr_sum.at[slot, there],
            gr_own.at[zh],
            s_gr2.at[slot, there],
            r_gr2.at[zh],
            device(y, mine, zl, owner, there),
            jnp.logical_and(on_own_path, jnp.logical_and(owner == zl, there == core)),
        )

    for phase in range(side):
        partials_left(phase)

    order = sorted(range(side), key=lambda step: min(step, side - step))
    for step in order:
        who = (x + step) % side
        if step > 0:
            for there in range(2):
                arrived(gtri.at[who, there], r_gtri.at[who, there])
                widen(who, there)
        arrived(left_x.at[who], r_left_x.at[who])

        def right_block(index, carry, step=step, who=who):
            slot = index // 2
            part = index % 2
            if step == 0:
                sums = nothing
            else:
                sums = [gr_acc[index, a] for a in range(16)]
            sums = products(
                sums,
                lambda n: left_x[who, slot, n // 8, n % 8],
                lambda n, a: gtri_float[who, n // 8, pl.ds(n % 8 * 16 + part * 8 + a, 1)],
            )
            if step == order[-1]:
                for a in range(8):
                    gr_sum[slot, part, a] = jnp.concatenate(
                        [sums[a], sums[a + 8]], axis=0
                    ).astype(BF16)
                push(*fourth_right(slot, part))
            else:
                for a in range(16):
                    gr_acc[index, a] = sums[a]
            return carry

        lax.fori_loop(0, 2 * half, right_block, 0)

    def sums_left(phase):
        slot, there = turn_of(phase)
        for step in range(1, side):
            who = (y + step) % side
            arrived(gl_in.at[who, slot, there], r_gl1.at[who, slot, there])
        value = gl_part[y, slot, there].astype(F32)
        for step in range(1, side):
            value = value + gl_in[(y + step) % side, slot, there].astype(F32)
        gl_sum[slot, there] = value.astype(BF16)
        push(*fourth_left(slot, there))

    for phase in range(side):
        sums_left(phase)

    def total_of(own, sems):
        value = None
        for there in range(side):
            arrived(own.at[there], sems.at[there])
            term = own[there].astype(F32)
            value = term if value is None else value + term
        return value.reshape(128, 128)

    grad_left = total_of(gl_own, r_gl2)
    sig_a = saved[1]
    value_a = saved[2]
    masked = grad_left * mask_wide
    proj_0 = (masked * value_a * sig_a * (1.0 - sig_a)).astype(BF16)
    proj_1 = (masked * sig_a).astype(BF16)
    grad_right = total_of(gr_own, r_gr2)
    sig_b = saved[3]
    value_b = saved[4]
    masked = grad_right * mask_wide
    proj_2 = (masked * value_b * sig_b * (1.0 - sig_b)).astype(BF16)
    proj_3 = (masked * sig_b).astype(BF16)
    grad_proj = jnp.concatenate([proj_0, proj_1, proj_2, proj_3], axis=-1)
    grad_inputs = dot_nt(grad_proj, in_weight_ref[...]) + saved[9]
    result = saved[8] + norm_back(grad_inputs, saved[0], saved[7], norm_gain_ref[...])
    out_ref[...] = result.astype(BF16).reshape(8, 16, 128)

    for there in range(side):
        drain(*first_right(there))
        drain(*first_left(there))
    for there in range(2):
        drain(*labels_to(there))
        drain(*logits_to(there))
    tri_copy().wait_send()
    for step in range(1, side):
        left_to(step).wait_send()
    for step in range(1, 2 * side):
        gtri_to(step).wait_send()
    for slot in range(half):
        for step in range(1, side):
            second_left(slot, step).wait_send()
        for there in range(2):
            for step in range(1, side):
                second_right(slot, there, step).wait_send()
                third_left(slot, there, step).wait_send()
            drain(*fourth_left(slot, there))
            drain(*fourth_right(slot, there))


def local(
    pair,
    labels,
    residue_mask,
    norm_gain,
    in_weight,
    gate_weight,
    hidden_gain,
    out_weight,
    bin_weight,
):
    side = lax.axis_size("section")
    half = side // 2
    tile = (8, 16, 128)
    sems = [
        (side,),
        (side,),
        (half, side - 1),
        (half, 2, side - 1),
        (1,),
        (2,),
        (2,),
        (side - 1,),
        (2 * side - 1,),
        (half, 2, side - 1),
        (half, 2),
        (half, 2),
        (half, 2),
        (half, 2),
        (side, half),
        (side, half, 2),
        (1,),
        (2,),
        (2,),
        (side,),
        (side, 2),
        (side, half, 2),
        (side,),
        (side,),
    ]
    gathered = pltpu.VMEM((side, half, 2) + tile, BF16)
    residues = residue_mask.shape[0]
    if residues < 256:
        residue_mask = jnp.pad(residue_mask, (0, 256 - residues))
    return pl.pallas_call(
        functools.partial(kernel, side),
        out_shape=jax.ShapeDtypeStruct(tile, BF16),
        in_specs=[pl.BlockSpec(memory_space=pl.ANY)] * 9,
        out_specs=pl.BlockSpec(memory_space=pltpu.VMEM),
        scratch_shapes=[
            pltpu.VMEM(tile, BF16),
            pltpu.VMEM((8, 16), jnp.int32),
            pltpu.VMEM((1, 256), jnp.int32),
            pltpu.VMEM((1, 128), F32),
            pltpu.VMEM(in_weight.shape, BF16),
            pltpu.VMEM(gate_weight.shape, BF16),
            pltpu.VMEM((1, 128), F32),
            pltpu.VMEM(out_weight.shape, BF16),
            pltpu.VMEM(bin_weight.shape[::-1], BF16),
            pltpu.SemaphoreType.DMA((9,)),
            pltpu.VMEM(tile, BF16),
            pltpu.VMEM(tile, BF16),
            gathered,
            gathered,
            pltpu.VMEM((256, 8, 128), F32),
            pltpu.VMEM((2, 128, 128), F32),
            pltpu.VMEM((128, 128), F32),
            pltpu.VMEM((2, 64, 64), BF16),
            pltpu.VMEM((2, 64, 64), BF16),
            pltpu.VMEM((8, 16), F32),
            pltpu.VMEM((2, 8, 16), F32),
            gathered,
            pltpu.VMEM((side, 2, 128, 128), BF16),
            pltpu.VMEM((side, 2, 128, 128), F32),
            gathered,
            gathered,
            pltpu.VMEM((2 * half, 16, 8, 128), F32),
            pltpu.VMEM((half, 2) + tile, BF16),
            pltpu.VMEM((half, 2) + tile, BF16),
            pltpu.VMEM((side,) + tile, BF16),
            pltpu.VMEM((side,) + tile, BF16),
            pltpu.VMEM((10, 128, 128), F32),
        ]
        + [pltpu.SemaphoreType.DMA(shape) for shape in sems],
        compiler_params=pltpu.CompilerParams(
            collective_id=0, has_side_effects=True, vmem_limit_bytes=60 * 1024 * 1024
        ),
    )(
        pair,
        labels,
        residue_mask[None, :],
        norm_gain[None, :],
        in_weight,
        gate_weight,
        hidden_gain[None, :],
        out_weight,
        bin_weight.T,
    )


def solution(mesh):
    placed = (
        P(("section", "row"), "col", None),
        P(("section", "row"), "col"),
        P(),
        P(),
        P(),
        P(),
        P(),
        P(),
        P(),
    )
    return jax.shard_map(
        local,
        mesh=mesh,
        in_specs=placed,
        out_specs=P(("section", "row"), "col", None),
        check_vma=False,
    )
```

```python
import functools

import jax
import jax.numpy as jnp
from jax import lax
from jax.experimental import pallas as pl
from jax.experimental.pallas import tpu as pltpu
from jax.sharding import PartitionSpec as P

MESH = pl.DeviceIdType.MESH
F32 = jnp.float32
BF16 = jnp.bfloat16


def norm_parts(values, gain):
    centre = values - jnp.mean(values, axis=-1, keepdims=True)
    inverse = lax.rsqrt(jnp.mean(centre * centre, axis=-1, keepdims=True) + 1e-05)
    normed = centre * inverse
    return (normed, inverse, normed * gain)


def norm_back(upstream, normed, inverse, gain):
    scaled = upstream * gain
    return inverse * (
        scaled
        - jnp.mean(scaled, axis=-1, keepdims=True)
        - normed * jnp.mean(scaled * normed, axis=-1, keepdims=True)
    )


def dot_nt(a, b):
    return lax.dot_general(a, b, (((1,), (1,)), ((), ())), preferred_element_type=F32)


def kernel(
    side,
    pair_hbm,
    labels_hbm,
    mask_hbm,
    norm_gain_hbm,
    in_weight_hbm,
    gate_weight_hbm,
    hidden_gain_hbm,
    out_weight_hbm,
    bin_weight_hbm,
    out_ref,
    pair_ref,
    labels_ref,
    mask_ref,
    norm_gain_ref,
    in_weight_ref,
    gate_weight_ref,
    hidden_gain_ref,
    out_weight_ref,
    bin_weight_ref,
    loaded,
    left_own,
    right_own,
    left_all,
    right_all,
    acc,
    tri_part,
    tri_in,
    logit_out,
    logit_in,
    label_out,
    label_in,
    left_x,
    gtri,
    gtri_float,
    gl_part,
    gl_in,
    gr_acc,
    gl_sum,
    gr_sum,
    gl_own,
    gr_own,
    saved,
    s_left1,
    s_right1,
    s_left2,
    s_right2,
    s_tri,
    s_logit,
    s_label,
    s_left_x,
    s_gtri,
    s_gl1,
    s_gl2,
    s_gr2,
    r_left1,
    r_right1,
    r_left2,
    r_right2,
    r_tri,
    r_logit,
    r_label,
    r_left_x,
    r_gtri,
    r_gl1,
    r_gl2,
    r_gr2,
):
    half = side // 2
    x = lax.axis_index("section")
    row = lax.axis_index("row")
    col = lax.axis_index("col")
    zh = row // 2
    core = row % 2
    y = col // side
    zl = col % side
    my_k_core = zl // half
    my_k_slot = zl % half
    diagonal = jnp.logical_and(x == y, zh == zl)

    def turned(a, b):
        return (2 * a + side // 2 - b + side) % side

    mine = turned(y, x)
    meet = turned(x, y)

    def device(dx, dy, dzh, dzl, dcore):
        return (dx, dzh * 2 + dcore, dy * side + dzl)

    def send(src, dst, send_sem, recv_sem, target):
        return pltpu.make_async_remote_copy(
            src_ref=src,
            dst_ref=dst,
            send_sem=send_sem,
            recv_sem=recv_sem,
            device_id=target,
            device_id_type=MESH,
        )

    def push(src, dst, send_sem, recv_sem, target, is_self):
        @pl.when(is_self)
        def _():
            pltpu.make_async_copy(src, dst, recv_sem).start()

        @pl.when(jnp.logical_not(is_self))
        def _():
            send(src, dst, send_sem, recv_sem, target).start()

    def drain(src, dst, send_sem, recv_sem, target, is_self):
        @pl.when(jnp.logical_not(is_self))
        def _():
            send(src, dst, send_sem, recv_sem, target).wait_send()

    def arrived(ref, sem):
        pltpu.make_async_copy(ref, ref, sem).wait()

    barrier = pltpu.get_barrier_semaphore()

    operands = (
        (pair_hbm, pair_ref),
        (in_weight_hbm, in_weight_ref),
        (mask_hbm, mask_ref),
        (norm_gain_hbm, norm_gain_ref),
        (labels_hbm, labels_ref),
        (gate_weight_hbm, gate_weight_ref),
        (hidden_gain_hbm, hidden_gain_ref),
        (out_weight_hbm, out_weight_ref),
        (bin_weight_hbm, bin_weight_ref),
    )

    def load(index):
        return pltpu.make_async_copy(*operands[index], loaded.at[index])

    def greet(target, is_self=None):
        def signal():
            pl.semaphore_signal(barrier, inc=1, device_id=target, device_id_type=MESH)

        if is_self is None:
            signal()
        else:
            pl.when(jnp.logical_not(is_self))(signal)

    for index in range(9):
        load(index).start()

    on_own_path = jnp.logical_and(
        jnp.logical_and(x == y, meet == x), jnp.logical_and(zh == zl, core == my_k_core)
    )
    for slot in range(half):
        for there in range(2):
            source = core * half + slot
            greet(
                device(y, mine, zl, source, there),
                jnp.logical_and(on_own_path, jnp.logical_and(source == zl, there == core)),
            )
    for slot in range(half):
        for there in range(2):
            source = core * half + slot
            greet(
                device(x, y, zh, source, there),
                jnp.logical_and(source == zl, there == core),
            )
    greet(device(x, y, zh, zl, 1 - core))
    for step in range(1, side):
        greet(device(x, (y + step) % side, zh, zl, core))
        greet(device((x + step) % side, y, zh, zl, core))
        greet(device((x + step) % side, y, zh, zl, 1 - core))
    greetings = 2 * side + 1 + 3 * (side - 1)
    awaited = (
        greetings - on_own_path.astype(jnp.int32) - (core == my_k_core).astype(jnp.int32)
    )

    load(2).wait()
    place = lax.broadcasted_iota(jnp.int32, (128, 256), 0)
    lane = lax.broadcasted_iota(jnp.int32, (128, 256), 1)
    mask_float = mask_ref[...].astype(F32)
    first_row = (x * side + zh) * 16 + core * 8
    first_col = col * 16
    mask_i = jnp.sum(
        jnp.where(lane == first_row + place // 16, mask_float, 0.0), axis=1, keepdims=True
    )
    mask_j = jnp.sum(
        jnp.where(lane == first_col + place % 16, mask_float, 0.0), axis=1, keepdims=True
    )
    pair_mask = mask_i * mask_j
    load(0).wait()
    load(3).wait()
    pair_float = pair_ref[...].astype(F32).reshape(128, 128)
    normed_in, inverse_in, scaled_in = norm_parts(pair_float, norm_gain_ref[...])
    inputs = scaled_in.astype(BF16)
    load(1).wait()

    def projected(first):
        both = jnp.dot(
            inputs, in_weight_ref[:, first : first + 256], preferred_element_type=F32
        )
        return jax.nn.sigmoid(both[:, 0:128]), both[:, 128:256]

    sig_b, value_b = projected(256)
    right_own[...] = (sig_b * value_b * pair_mask).astype(BF16).reshape(8, 16, 128)
    pl.semaphore_wait(barrier, awaited)

    def first_right(there):
        return (
            right_own,
            right_all.at[y, my_k_slot, core],
            s_right1.at[there],
            r_right1.at[my_k_slot, core],
            device(meet, x, there, zh, my_k_core),
            jnp.logical_and(on_own_path, there == zh),
        )

    def first_left(there):
        return (
            left_own,
            left_all.at[y, my_k_slot, core],
            s_left1.at[there],
            r_left1.at[my_k_slot, core],
            device(x, y, zh, there, my_k_core),
            jnp.logical_and(there == zl, core == my_k_core),
        )

    def labels_to(there):
        return (
            label_out,
            label_in.at[core],
            s_label.at[there],
            r_label.at[core],
            device(y, x, zl, zh, there),
            jnp.logical_and(diagonal, there == core),
        )

    near = zh == 0
    push(*first_right(0))

    @pl.when(near)
    def _():
        for there in range(1, side):
            push(*first_right(there))

    sig_a, value_a = projected(0)
    left_own[...] = (sig_a * value_a * pair_mask).astype(BF16).reshape(8, 16, 128)
    push(*first_left(0))

    @pl.when(near)
    def _():
        for there in range(1, side):
            push(*first_left(there))

    @pl.when(jnp.logical_not(near))
    def _():
        drain(*first_left(0))
        for there in range(1, side):
            push(*first_left(there))
            push(*first_right(there))
        drain(*first_right(0))

    load(4).wait()
    label_out[...] = labels_ref[...].astype(F32)
    for index in range(5, 9):
        load(index).wait()

    saved[0] = normed_in
    saved[1] = value_a * pair_mask * sig_a * (1.0 - sig_a)
    saved[2] = sig_a * pair_mask
    saved[3] = value_b * pair_mask * sig_b * (1.0 - sig_b)
    saved[4] = sig_b * pair_mask
    saved[5] = jax.nn.sigmoid(jnp.dot(inputs, gate_weight_ref[...], preferred_element_type=F32))
    saved[6] = jnp.broadcast_to(pair_mask, (128, 128))
    saved[7] = jnp.broadcast_to(inverse_in, (128, 128))

    def second_left(slot, step):
        return send(
            left_all.at[y, slot],
            left_all.at[y, slot],
            s_left2.at[slot, step - 1],
            r_left2.at[y, slot],
            device(x, (y + step) % side, zh, zl, core),
        )

    def turn_of(phase):
        return phase // 2, phase % 2

    def second_right(slot, part, step):
        return send(
            right_all.at[mine, slot, part],
            right_all.at[mine, slot, part],
            s_right2.at[slot, part, step - 1],
            r_right2.at[mine, slot, part],
            device((x + step) % side, y, zh, zl, core),
        )

    for slot in range(half):
        for there in range(2):
            arrived(left_all.at[y, slot, there], r_left1.at[slot, there])
        for step in range(1, side):
            second_left(slot, step).start()

    def forward(phase):
        slot, part = turn_of(phase)
        arrived(right_all.at[mine, slot, part], r_right1.at[slot, part])
        for step in range(1, side):
            second_right(slot, part, step).start()

    acc[...] = jnp.zeros_like(acc)

    def tri_blocks(i_half, slot, j_half):
        def body(index, carry):
            i_low = index // 2 * 4
            j_low = index % 2 * 4
            base = (i_half * 8 + i_low) * 16 + j_half * 8 + j_low
            sums = [[acc[base + a * 16 + b] for b in range(4)] for a in range(4)]
            for who in range(side):
                lefts = [left_all[who, slot, i_half, i_low + a].astype(F32) for a in range(4)]
                rights = [right_all[who, slot, j_half, j_low + b].astype(F32) for b in range(4)]
                for a in range(4):
                    for b in range(4):
                        product = lefts[a] * rights[b]
                        sums[a][b] = sums[a][b] + (product[0:8] + product[8:16])
            for a in range(4):
                for b in range(4):
                    acc[base + a * 16 + b] = sums[a][b]
            return carry

        lax.fori_loop(0, 4, body, 0)

    def fold(part):
        def body(index, carry):
            at = part * 128 + index * 8
            tri_part[part, pl.ds(index * 8, 8)] = jnp.sum(acc[pl.ds(at, 8)], axis=1)
            return carry

        lax.fori_loop(0, 16, body, 0)

    def tri_copy():
        return send(
            tri_part.at[1 - core],
            tri_in,
            s_tri.at[0],
            r_tri.at[0],
            device(x, y, zh, zl, 1 - core),
        )

    forward(0)
    for phase in range(side):
        if phase < side - 1:
            forward(phase + 1)
        slot, part = turn_of(phase)
        if phase == 0:
            for step in range(1, side):
                for there in range(half):
                    who = (y + step) % side
                    arrived(left_all.at[who, there], r_left2.at[who, there])
        for step in range(1, side):
            who = (mine + step) % side
            arrived(right_all.at[who, slot, part], r_right2.at[who, slot, part])
        tri_blocks(1 - core, slot, part)
        if phase == side - 1:
            fold(1 - core)
            tri_copy().start()
        tri_blocks(core, slot, part)
    fold(core)
    arrived(tri_in, r_tri.at[0])
    for there in range(2):
        push(*labels_to(there))
    triangle = tri_part[core] + tri_in[...]

    hidden_gain = hidden_gain_ref[...]
    normed_t, inverse_t, scaled_t = norm_parts(triangle, hidden_gain)
    update = jnp.dot(scaled_t.astype(BF16), out_weight_ref[...], preferred_element_type=F32)
    gate_out = saved[5]
    pair_out = (pair_ref[...].astype(F32).reshape(128, 128) + gate_out * update).astype(BF16)
    logits = dot_nt(pair_out, bin_weight_ref[...])
    logits = logits.astype(BF16).astype(F32)
    blocks = logits.reshape(8, 2, 8, 64)
    for there in range(2):
        logit_out[there] = blocks[:, there].reshape(64, 64).astype(BF16)

    def logits_to(there):
        return (
            logit_out.at[there],
            logit_in.at[core],
            s_logit.at[there],
            r_logit.at[core],
            device(y, x, zl, zh, there),
            jnp.logical_and(diagonal, there == core),
        )

    for there in range(2):
        push(*logits_to(there))

    def left_to(step):
        who = (x + step) % side
        return send(
            left_all.at[turned(y, who)],
            left_x.at[x],
            s_left_x.at[step - 1],
            r_left_x.at[x],
            device(who, y, zh, zl, core),
        )

    for step in range(1, side):
        left_to(step).start()
    pltpu.make_async_copy(left_all.at[mine], left_x.at[x], r_left_x.at[x]).start()

    for there in range(2):
        arrived(label_in.at[there], r_label.at[there])
    place16 = lax.broadcasted_iota(jnp.int32, (128, 16), 0)
    lane16 = lax.broadcasted_iota(jnp.int32, (128, 16), 1)
    place8 = lax.broadcasted_iota(jnp.int32, (128, 8), 0)
    lane8 = lax.broadcasted_iota(jnp.int32, (128, 8), 1)
    spread = jnp.dot(
        (lane8 == place8 // 16).astype(F32), label_out[...], preferred_element_type=F32
    )
    label = jnp.sum(jnp.where(lane16 == place16 % 16, spread, 0.0), axis=1, keepdims=True)
    spread = jnp.dot(
        (lane16 == place16 % 16).astype(F32),
        label_in[...].reshape(16, 16),
        preferred_element_type=F32,
    )
    label_mirror = jnp.sum(
        jnp.where(lane16 == core * 8 + place16 // 16, spread, 0.0), axis=1, keepdims=True
    )
    bins = lax.broadcasted_iota(jnp.int32, (128, 64), 1)
    onehot = (label.astype(jnp.int32) == bins).astype(F32)
    onehot_mirror = (label_mirror.astype(jnp.int32) == bins).astype(F32)
    at_row = lax.broadcasted_iota(jnp.int32, (128, 128), 0)
    at_lane = lax.broadcasted_iota(jnp.int32, (128, 128), 1)
    turn = at_lane == (at_row // 8) % 2 * 64 + at_row % 8 * 8 + at_row // 16
    turn = turn.astype(F32).astype(BF16)
    mask_wide = saved[6]
    pair_mask = mask_wide[:, 0:64]

    for there in range(2):
        arrived(logit_in.at[there], r_logit.at[there])
    mirrored = jnp.dot(turn, logit_in[...].reshape(128, 64), preferred_element_type=F32)
    weights = jnp.exp(logits + mirrored)
    probs = weights / jnp.sum(weights, axis=-1, keepdims=True)
    grad_bins = (pair_mask * (probs - onehot)).astype(BF16).astype(F32)
    grad_mirror = (pair_mask * (probs - onehot_mirror)).astype(BF16).astype(F32)
    grad_sym = (grad_bins + grad_mirror).astype(BF16)
    grad_out = jnp.dot(grad_sym, bin_weight_ref[...], preferred_element_type=F32)
    grad_update = (grad_out * gate_out).astype(BF16)
    grad_scaled = dot_nt(grad_update, out_weight_ref[...])
    grad_triangle = norm_back(grad_scaled, normed_t, inverse_t, hidden_gain)
    gtri[x, core] = grad_triangle.astype(BF16)

    def gtri_to(step):
        other = (x * 2 + core + step) % (2 * side)
        return send(
            gtri.at[x, core],
            gtri.at[x, core],
            s_gtri.at[step - 1],
            r_gtri.at[x, core],
            device(other // 2, y, zh, zl, other % 2),
        )

    for step in range(1, 2 * side):
        gtri_to(step).start()
    grad_gate = (grad_out * update * gate_out * (1.0 - gate_out)).astype(BF16)
    saved[8] = grad_out
    saved[9] = dot_nt(grad_gate, gate_weight_ref[...])

    def widen(who, part):
        gtri_float[who, part] = gtri[who, part].astype(F32)

    widen(x, core)
    arrived(gtri.at[x, 1 - core], r_gtri.at[x, 1 - core])
    widen(x, 1 - core)

    def products(sums, tile_of, factor_of):
        low, high = list(sums[0:8]), list(sums[8:16])
        for n in range(16):
            tile = tile_of(n).astype(F32)
            for a in range(8):
                factor = jnp.broadcast_to(factor_of(n, a), (8, 128))
                low[a] = low[a] + factor * tile[0:8]
                high[a] = high[a] + factor * tile[8:16]
        return low + high

    nothing = [jnp.zeros((8, 128), F32) for _ in range(16)]

    def partial_left(who, slot, part):
        sums = products(
            nothing,
            lambda n: right_all[who, slot, n // 8, n % 8],
            lambda n, a: gtri_float[x, part, pl.ds(a * 16 + n, 1)],
        )
        for a in range(8):
            gl_part[who, slot, part, a] = jnp.concatenate(
                [sums[a], sums[a + 8]], axis=0
            ).astype(BF16)

    def third_left(slot, part, step):
        who = (y + step) % side
        return send(
            gl_part.at[who, slot, part],
            gl_in.at[y, slot, part],
            s_gl1.at[slot, part, step - 1],
            r_gl1.at[y, slot, part],
            device(x, who, zh, zl, core),
        )

    def partials_left(phase):
        slot, part = turn_of(phase)

        def body(step, carry):
            partial_left((y + step) % side, slot, part)

            @pl.when(step < side)
            def _():
                third_left(slot, part, step).start()

            return carry

        lax.fori_loop(1, side + 1, body, 0)

    def fourth_left(slot, there):
        owner = core * half + slot
        return (
            gl_sum.at[slot, there],
            gl_own.at[zl],
            s_gl2.at[slot, there],
            r_gl2.at[zl],
            device(x, y, zh, owner, there),
            jnp.logical_and(owner == zl, there == core),
        )

    def fourth_right(slot, there):
        owner = core * half + slot
        return (
            gr_sum.at[slot, there],
            gr_own.at[zh],
            s_gr2.at[slot, there],
            r_gr2.at[zh],
            device(y, mine, zl, owner, there),
            jnp.logical_and(on_own_path, jnp.logical_and(owner == zl, there == core)),
        )

    for phase in range(side):
        partials_left(phase)

    order = sorted(range(side), key=lambda step: min(step, side - step))
    for step in order:
        who = (x + step) % side
        if step > 0:
            for there in range(2):
                arrived(gtri.at[who, there], r_gtri.at[who, there])
                widen(who, there)
        arrived(left_x.at[who], r_left_x.at[who])

        def right_block(index, carry, step=step, who=who):
            slot = index // 2
            part = 1 - index % 2
            if step == 0:
                sums = nothing
            else:
                sums = [gr_acc[index, a] for a in range(16)]
            sums = products(
                sums,
                lambda n: left_x[who, slot, n // 8, n % 8],
                lambda n, a: gtri_float[who, n // 8, pl.ds(n % 8 * 16 + part * 8 + a, 1)],
            )
            if step == order[-1]:
                for a in range(8):
                    gr_sum[slot, part, a] = jnp.concatenate(
                        [sums[a], sums[a + 8]], axis=0
                    ).astype(BF16)
                push(*fourth_right(slot, part))
            else:
                for a in range(16):
                    gr_acc[index, a] = sums[a]
            return carry

        lax.fori_loop(0, 2 * half, right_block, 0)

    def sums_left(phase):
        slot, there = turn_of(phase)
        for step in range(1, side):
            who = (y + step) % side
            arrived(gl_in.at[who, slot, there], r_gl1.at[who, slot, there])
        value = gl_part[y, slot, there].astype(F32)
        for step in range(1, side):
            value = value + gl_in[(y + step) % side, slot, there].astype(F32)
        gl_sum[slot, there] = value.astype(BF16)
        push(*fourth_left(slot, there))

    for phase in range(side):
        sums_left(phase)

    def total_of(own, sems):
        value = None
        for there in range(side):
            arrived(own.at[there], sems.at[there])
            term = own[there].astype(F32)
            value = term if value is None else value + term
        return value.reshape(128, 128)

    def project(grad, first):
        grad_proj = jnp.concatenate(
            [(grad * saved[first]).astype(BF16), (grad * saved[first + 1]).astype(BF16)], axis=-1
        )
        columns = (first - 1) * 128
        return dot_nt(grad_proj, in_weight_ref[:, columns : columns + 256])

    grad_inputs = saved[9] + project(total_of(gl_own, r_gl2), 1)
    grad_inputs = grad_inputs + project(total_of(gr_own, r_gr2), 3)
    result = saved[8] + norm_back(grad_inputs, saved[0], saved[7], norm_gain_ref[...])
    out_ref[...] = result.astype(BF16).reshape(8, 16, 128)

    @pl.when(near)
    def _():
        drain(*first_right(0))
        drain(*first_left(0))

    for there in range(1, side):
        drain(*first_right(there))
        drain(*first_left(there))
    for there in range(2):
        drain(*labels_to(there))
        drain(*logits_to(there))
    tri_copy().wait_send()
    for step in range(1, side):
        left_to(step).wait_send()
    for step in range(1, 2 * side):
        gtri_to(step).wait_send()
    for slot in range(half):
        for step in range(1, side):
            second_left(slot, step).wait_send()
        for there in range(2):
            for step in range(1, side):
                second_right(slot, there, step).wait_send()
                third_left(slot, there, step).wait_send()
            drain(*fourth_left(slot, there))
            drain(*fourth_right(slot, there))


def local(
    pair,
    labels,
    residue_mask,
    norm_gain,
    in_weight,
    gate_weight,
    hidden_gain,
    out_weight,
    bin_weight,
):
    side = lax.axis_size("section")
    half = side // 2
    tile = (8, 16, 128)
    sems = [
        (side,),
        (side,),
        (half, side - 1),
        (half, 2, side - 1),
        (1,),
        (2,),
        (2,),
        (side - 1,),
        (2 * side - 1,),
        (half, 2, side - 1),
        (half, 2),
        (half, 2),
        (half, 2),
        (half, 2),
        (side, half),
        (side, half, 2),
        (1,),
        (2,),
        (2,),
        (side,),
        (side, 2),
        (side, half, 2),
        (side,),
        (side,),
    ]
    gathered = pltpu.VMEM((side, half, 2) + tile, BF16)
    residues = residue_mask.shape[0]
    if residues < 256:
        residue_mask = jnp.pad(residue_mask, (0, 256 - residues))
    return pl.pallas_call(
        functools.partial(kernel, side),
        out_shape=jax.ShapeDtypeStruct(tile, BF16),
        in_specs=[pl.BlockSpec(memory_space=pl.ANY)] * 9,
        out_specs=pl.BlockSpec(memory_space=pltpu.VMEM),
        scratch_shapes=[
            pltpu.VMEM(tile, BF16),
            pltpu.VMEM((8, 16), jnp.int32),
            pltpu.VMEM((1, 256), jnp.int32),
            pltpu.VMEM((1, 128), F32),
            pltpu.VMEM(in_weight.shape, BF16),
            pltpu.VMEM(gate_weight.shape, BF16),
            pltpu.VMEM((1, 128), F32),
            pltpu.VMEM(out_weight.shape, BF16),
            pltpu.VMEM(bin_weight.shape[::-1], BF16),
            pltpu.SemaphoreType.DMA((9,)),
            pltpu.VMEM(tile, BF16),
            pltpu.VMEM(tile, BF16),
            gathered,
            gathered,
            pltpu.VMEM((256, 8, 128), F32),
            pltpu.VMEM((2, 128, 128), F32),
            pltpu.VMEM((128, 128), F32),
            pltpu.VMEM((2, 64, 64), BF16),
            pltpu.VMEM((2, 64, 64), BF16),
            pltpu.VMEM((8, 16), F32),
            pltpu.VMEM((2, 8, 16), F32),
            gathered,
            pltpu.VMEM((side, 2, 128, 128), BF16),
            pltpu.VMEM((side, 2, 128, 128), F32),
            gathered,
            gathered,
            pltpu.VMEM((2 * half, 16, 8, 128), F32),
            pltpu.VMEM((half, 2) + tile, BF16),
            pltpu.VMEM((half, 2) + tile, BF16),
            pltpu.VMEM((side,) + tile, BF16),
            pltpu.VMEM((side,) + tile, BF16),
            pltpu.VMEM((10, 128, 128), F32),
        ]
        + [pltpu.SemaphoreType.DMA(shape) for shape in sems],
        compiler_params=pltpu.CompilerParams(
            collective_id=0, has_side_effects=True, vmem_limit_bytes=60 * 1024 * 1024
        ),
    )(
        pair,
        labels,
        residue_mask[None, :],
        norm_gain[None, :],
        in_weight,
        gate_weight,
        hidden_gain[None, :],
        out_weight,
        bin_weight.T,
    )


def solution(mesh):
    placed = (
        P(("section", "row"), "col", None),
        P(("section", "row"), "col"),
        P(),
        P(),
        P(),
        P(),
        P(),
        P(),
        P(),
    )
    return jax.shard_map(
        local,
        mesh=mesh,
        in_specs=placed,
        out_specs=P(("section", "row"), "col", None),
        check_vma=False,
    )
```

```python
import functools

import jax
import jax.numpy as jnp
from jax import lax
from jax.experimental import pallas as pl
from jax.experimental.pallas import tpu as pltpu
from jax.sharding import PartitionSpec as P

MESH = pl.DeviceIdType.MESH
F32 = jnp.float32
BF16 = jnp.bfloat16


def norm_parts(values, gain):
    centre = values - jnp.mean(values, axis=-1, keepdims=True)
    inverse = lax.rsqrt(jnp.mean(centre * centre, axis=-1, keepdims=True) + 1e-05)
    normed = centre * inverse
    return (normed, inverse, normed * gain)


def norm_back(upstream, normed, inverse, gain):
    scaled = upstream * gain
    return inverse * (
        scaled
        - jnp.mean(scaled, axis=-1, keepdims=True)
        - normed * jnp.mean(scaled * normed, axis=-1, keepdims=True)
    )


def dot_nt(a, b):
    return lax.dot_general(a, b, (((1,), (1,)), ((), ())), preferred_element_type=F32)


def kernel(
    side,
    pair_hbm,
    labels_hbm,
    mask_hbm,
    norm_gain_hbm,
    in_weight_hbm,
    gate_weight_hbm,
    hidden_gain_hbm,
    out_weight_hbm,
    bin_weight_hbm,
    out_ref,
    pair_ref,
    labels_ref,
    mask_ref,
    norm_gain_ref,
    in_weight_ref,
    gate_weight_ref,
    hidden_gain_ref,
    out_weight_ref,
    bin_weight_ref,
    loaded,
    left_own,
    right_own,
    left_all,
    right_all,
    acc,
    tri_part,
    tri_in,
    logit_out,
    logit_in,
    label_out,
    label_in,
    left_x,
    gtri,
    gtri_float,
    gl_part,
    gl_in,
    gr_acc,
    gl_sum,
    gr_sum,
    gl_own,
    gr_own,
    saved,
    s_left1,
    s_right1,
    s_left2,
    s_right2,
    s_tri,
    s_logit,
    s_label,
    s_left_x,
    s_gtri,
    s_gl1,
    s_gl2,
    s_gr2,
    r_left1,
    r_right1,
    r_left2,
    r_right2,
    r_tri,
    r_logit,
    r_label,
    r_left_x,
    r_gtri,
    r_gl1,
    r_gl2,
    r_gr2,
):
    half = side // 2
    x = lax.axis_index("section")
    row = lax.axis_index("row")
    col = lax.axis_index("col")
    zh = row // 2
    core = row % 2
    y = col // side
    zl = col % side
    my_k_core = zl // half
    my_k_slot = zl % half
    diagonal = jnp.logical_and(x == y, zh == zl)

    def turned(a, b):
        return (2 * a + side // 2 - b + side) % side

    mine = turned(y, x)
    meet = turned(x, y)

    def device(dx, dy, dzh, dzl, dcore):
        return (dx, dzh * 2 + dcore, dy * side + dzl)

    def send(src, dst, send_sem, recv_sem, target):
        return pltpu.make_async_remote_copy(
            src_ref=src,
            dst_ref=dst,
            send_sem=send_sem,
            recv_sem=recv_sem,
            device_id=target,
            device_id_type=MESH,
        )

    def push(src, dst, send_sem, recv_sem, target, is_self):
        @pl.when(is_self)
        def _():
            pltpu.make_async_copy(src, dst, recv_sem).start()

        @pl.when(jnp.logical_not(is_self))
        def _():
            send(src, dst, send_sem, recv_sem, target).start()

    def drain(src, dst, send_sem, recv_sem, target, is_self):
        @pl.when(jnp.logical_not(is_self))
        def _():
            send(src, dst, send_sem, recv_sem, target).wait_send()

    def arrived(ref, sem):
        pltpu.make_async_copy(ref, ref, sem).wait()

    barrier = pltpu.get_barrier_semaphore()

    operands = (
        (pair_hbm, pair_ref),
        (in_weight_hbm, in_weight_ref),
        (mask_hbm, mask_ref),
        (norm_gain_hbm, norm_gain_ref),
        (labels_hbm, labels_ref),
        (gate_weight_hbm, gate_weight_ref),
        (hidden_gain_hbm, hidden_gain_ref),
        (out_weight_hbm, out_weight_ref),
        (bin_weight_hbm, bin_weight_ref),
    )

    def load(index):
        return pltpu.make_async_copy(*operands[index], loaded.at[index])

    def greet(target, is_self=None):
        def signal():
            pl.semaphore_signal(barrier, inc=1, device_id=target, device_id_type=MESH)

        if is_self is None:
            signal()
        else:
            pl.when(jnp.logical_not(is_self))(signal)

    for index in range(9):
        load(index).start()

    on_own_path = jnp.logical_and(
        jnp.logical_and(x == y, meet == x), jnp.logical_and(zh == zl, core == my_k_core)
    )
    for slot in range(half):
        for there in range(2):
            source = core * half + slot
            greet(
                device(y, mine, zl, source, there),
                jnp.logical_and(on_own_path, jnp.logical_and(source == zl, there == core)),
            )
    for slot in range(half):
        for there in range(2):
            source = core * half + slot
            greet(
                device(x, y, zh, source, there),
                jnp.logical_and(source == zl, there == core),
            )
    greet(device(x, y, zh, zl, 1 - core))
    for step in range(1, side):
        greet(device(x, (y + step) % side, zh, zl, core))
        greet(device((x + step) % side, y, zh, zl, core))
        greet(device((x + step) % side, y, zh, zl, 1 - core))
    greetings = 2 * side + 1 + 3 * (side - 1)
    awaited = (
        greetings - on_own_path.astype(jnp.int32) - (core == my_k_core).astype(jnp.int32)
    )

    load(2).wait()
    place = lax.broadcasted_iota(jnp.int32, (128, 256), 0)
    lane = lax.broadcasted_iota(jnp.int32, (128, 256), 1)
    mask_float = mask_ref[...].astype(F32)
    first_row = (x * side + zh) * 16 + core * 8
    first_col = col * 16
    mask_i = jnp.sum(
        jnp.where(lane == first_row + place // 16, mask_float, 0.0), axis=1, keepdims=True
    )
    mask_j = jnp.sum(
        jnp.where(lane == first_col + place % 16, mask_float, 0.0), axis=1, keepdims=True
    )
    pair_mask = mask_i * mask_j
    load(0).wait()
    load(3).wait()
    pair_float = pair_ref[...].astype(F32).reshape(128, 128)
    normed_in, inverse_in, scaled_in = norm_parts(pair_float, norm_gain_ref[...])
    inputs = scaled_in.astype(BF16)
    load(1).wait()

    def projected(first):
        both = jnp.dot(
            inputs, in_weight_ref[:, first : first + 256], preferred_element_type=F32
        )
        return jax.nn.sigmoid(both[:, 0:128]), both[:, 128:256]

    sig_b, value_b = projected(256)
    right_own[...] = (sig_b * value_b * pair_mask).astype(BF16).reshape(8, 16, 128)
    pl.semaphore_wait(barrier, awaited)

    def first_right(there):
        return (
            right_own,
            right_all.at[y, my_k_slot, core],
            s_right1.at[there],
            r_right1.at[my_k_slot, core],
            device(meet, x, there, zh, my_k_core),
            jnp.logical_and(on_own_path, there == zh),
        )

    def first_left(there):
        return (
            left_own,
            left_all.at[y, my_k_slot, core],
            s_left1.at[there],
            r_left1.at[my_k_slot, core],
            device(x, y, zh, there, my_k_core),
            jnp.logical_and(there == zl, core == my_k_core),
        )

    def labels_to(there):
        return (
            label_out,
            label_in.at[core],
            s_label.at[there],
            r_label.at[core],
            device(y, x, zl, zh, there),
            jnp.logical_and(diagonal, there == core),
        )

    near = zh == 0
    push(*first_right(0))

    @pl.when(near)
    def _():
        for there in range(1, side):
            push(*first_right(there))

    sig_a, value_a = projected(0)
    left_own[...] = (sig_a * value_a * pair_mask).astype(BF16).reshape(8, 16, 128)
    push(*first_left(0))

    @pl.when(near)
    def _():
        for there in range(1, side):
            push(*first_left(there))

    @pl.when(jnp.logical_not(near))
    def _():
        drain(*first_left(0))
        for there in range(1, side):
            push(*first_left(there))
            push(*first_right(there))
        drain(*first_right(0))

    load(4).wait()
    label_out[...] = labels_ref[...].astype(F32)
    for index in range(5, 9):
        load(index).wait()

    saved[0] = normed_in
    saved[1] = value_a * pair_mask * sig_a * (1.0 - sig_a)
    saved[2] = sig_a * pair_mask
    saved[3] = value_b * pair_mask * sig_b * (1.0 - sig_b)
    saved[4] = sig_b * pair_mask
    saved[5] = jax.nn.sigmoid(jnp.dot(inputs, gate_weight_ref[...], preferred_element_type=F32))
    saved[6] = jnp.broadcast_to(pair_mask, (128, 128))
    saved[7] = jnp.broadcast_to(inverse_in, (128, 128))

    def second_left(slot, step):
        return send(
            left_all.at[y, slot],
            left_all.at[y, slot],
            s_left2.at[slot, step - 1],
            r_left2.at[y, slot],
            device(x, (y + step) % side, zh, zl, core),
        )

    def turn_of(phase):
        return phase // 2, phase % 2

    def second_right(slot, step):
        return send(
            right_all.at[mine, slot],
            right_all.at[mine, slot],
            s_right2.at[slot, step - 1],
            r_right2.at[mine, slot],
            device((x + step) % side, y, zh, zl, core),
        )

    for slot in range(half):
        for there in range(2):
            arrived(left_all.at[y, slot, there], r_left1.at[slot, there])
        for step in range(1, side):
            second_left(slot, step).start()

    def forward(slot):
        for part in range(2):
            arrived(right_all.at[mine, slot, part], r_right1.at[slot, part])
        for step in range(1, side):
            second_right(slot, step).start()

    acc[...] = jnp.zeros_like(acc)

    def tri_blocks(i_half, slot, j_half):
        def body(index, carry):
            i_low = index // 2 * 4
            j_low = index % 2 * 4
            base = (i_half * 8 + i_low) * 16 + j_half * 8 + j_low
            sums = [[acc[base + a * 16 + b] for b in range(4)] for a in range(4)]
            for who in range(side):
                lefts = [left_all[who, slot, i_half, i_low + a].astype(F32) for a in range(4)]
                rights = [right_all[who, slot, j_half, j_low + b].astype(F32) for b in range(4)]
                for a in range(4):
                    for b in range(4):
                        product = lefts[a] * rights[b]
                        sums[a][b] = sums[a][b] + (product[0:8] + product[8:16])
            for a in range(4):
                for b in range(4):
                    acc[base + a * 16 + b] = sums[a][b]
            return carry

        lax.fori_loop(0, 4, body, 0)

    def fold(part):
        def body(index, carry):
            at = part * 128 + index * 8
            tri_part[part, pl.ds(index * 8, 8)] = jnp.sum(acc[pl.ds(at, 8)], axis=1)
            return carry

        lax.fori_loop(0, 16, body, 0)

    def tri_copy():
        return send(
            tri_part.at[1 - core],
            tri_in,
            s_tri.at[0],
            r_tri.at[0],
            device(x, y, zh, zl, 1 - core),
        )

    forward(0)
    for phase in range(side):
        if phase % 2 == 0 and phase // 2 + 1 < half:
            forward(phase // 2 + 1)
        slot, part = turn_of(phase)
        if phase == 0:
            for step in range(1, side):
                for there in range(half):
                    who = (y + step) % side
                    arrived(left_all.at[who, there], r_left2.at[who, there])
        for step in range(1, side):
            who = (mine + step) % side
            if part == 0:
                arrived(right_all.at[who, slot], r_right2.at[who, slot])
        tri_blocks(1 - core, slot, part)
        if phase == side - 1:
            fold(1 - core)
            tri_copy().start()
        tri_blocks(core, slot, part)
    fold(core)
    arrived(tri_in, r_tri.at[0])
    for there in range(2):
        push(*labels_to(there))
    triangle = tri_part[core] + tri_in[...]

    hidden_gain = hidden_gain_ref[...]
    normed_t, inverse_t, scaled_t = norm_parts(triangle, hidden_gain)
    update = jnp.dot(scaled_t.astype(BF16), out_weight_ref[...], preferred_element_type=F32)
    gate_out = saved[5]
    pair_out = (pair_ref[...].astype(F32).reshape(128, 128) + gate_out * update).astype(BF16)
    logits = dot_nt(pair_out, bin_weight_ref[...])
    logits = logits.astype(BF16).astype(F32)
    blocks = logits.reshape(8, 2, 8, 64)
    for there in range(2):
        logit_out[there] = blocks[:, there].reshape(64, 64).astype(BF16)

    def logits_to(there):
        return (
            logit_out.at[there],
            logit_in.at[core],
            s_logit.at[there],
            r_logit.at[core],
            device(y, x, zl, zh, there),
            jnp.logical_and(diagonal, there == core),
        )

    for there in range(2):
        push(*logits_to(there))

    def left_to(step):
        who = (x + step) % side
        return send(
            left_all.at[turned(y, who)],
            left_x.at[x],
            s_left_x.at[step - 1],
            r_left_x.at[x],
            device(who, y, zh, zl, core),
        )

    for step in range(1, side):
        left_to(step).start()
    pltpu.make_async_copy(left_all.at[mine], left_x.at[x], r_left_x.at[x]).start()

    for there in range(2):
        arrived(label_in.at[there], r_label.at[there])
    place16 = lax.broadcasted_iota(jnp.int32, (128, 16), 0)
    lane16 = lax.broadcasted_iota(jnp.int32, (128, 16), 1)
    place8 = lax.broadcasted_iota(jnp.int32, (128, 8), 0)
    lane8 = lax.broadcasted_iota(jnp.int32, (128, 8), 1)
    spread = jnp.dot(
        (lane8 == place8 // 16).astype(F32), label_out[...], preferred_element_type=F32
    )
    label = jnp.sum(jnp.where(lane16 == place16 % 16, spread, 0.0), axis=1, keepdims=True)
    spread = jnp.dot(
        (lane16 == place16 % 16).astype(F32),
        label_in[...].reshape(16, 16),
        preferred_element_type=F32,
    )
    label_mirror = jnp.sum(
        jnp.where(lane16 == core * 8 + place16 // 16, spread, 0.0), axis=1, keepdims=True
    )
    bins = lax.broadcasted_iota(jnp.int32, (128, 64), 1)
    onehot = (label.astype(jnp.int32) == bins).astype(F32)
    onehot_mirror = (label_mirror.astype(jnp.int32) == bins).astype(F32)
    at_row = lax.broadcasted_iota(jnp.int32, (128, 128), 0)
    at_lane = lax.broadcasted_iota(jnp.int32, (128, 128), 1)
    turn = at_lane == (at_row // 8) % 2 * 64 + at_row % 8 * 8 + at_row // 16
    turn = turn.astype(F32).astype(BF16)
    mask_wide = saved[6]
    pair_mask = mask_wide[:, 0:64]

    for there in range(2):
        arrived(logit_in.at[there], r_logit.at[there])
    mirrored = jnp.dot(turn, logit_in[...].reshape(128, 64), preferred_element_type=F32)
    weights = jnp.exp(logits + mirrored)
    probs = weights / jnp.sum(weights, axis=-1, keepdims=True)
    grad_bins = (pair_mask * (probs - onehot)).astype(BF16).astype(F32)
    grad_mirror = (pair_mask * (probs - onehot_mirror)).astype(BF16).astype(F32)
    grad_sym = (grad_bins + grad_mirror).astype(BF16)
    grad_out = jnp.dot(grad_sym, bin_weight_ref[...], preferred_element_type=F32)
    grad_update = (grad_out * gate_out).astype(BF16)
    grad_scaled = dot_nt(grad_update, out_weight_ref[...])
    grad_triangle = norm_back(grad_scaled, normed_t, inverse_t, hidden_gain)
    gtri[x, core] = grad_triangle.astype(BF16)

    def gtri_to(step):
        other = (x * 2 + core + step) % (2 * side)
        return send(
            gtri.at[x, core],
            gtri.at[x, core],
            s_gtri.at[step - 1],
            r_gtri.at[x, core],
            device(other // 2, y, zh, zl, other % 2),
        )

    for step in range(1, 2 * side):
        gtri_to(step).start()
    grad_gate = (grad_out * update * gate_out * (1.0 - gate_out)).astype(BF16)
    saved[8] = grad_out
    saved[9] = dot_nt(grad_gate, gate_weight_ref[...])

    def widen(who, part):
        gtri_float[who, part] = gtri[who, part].astype(F32)

    widen(x, core)
    arrived(gtri.at[x, 1 - core], r_gtri.at[x, 1 - core])
    widen(x, 1 - core)

    def products(sums, tile_of, factor_of):
        low, high = list(sums[0:8]), list(sums[8:16])
        for n in range(16):
            tile = tile_of(n).astype(F32)
            for a in range(8):
                factor = jnp.broadcast_to(factor_of(n, a), (8, 128))
                low[a] = low[a] + factor * tile[0:8]
                high[a] = high[a] + factor * tile[8:16]
        return low + high

    nothing = [jnp.zeros((8, 128), F32) for _ in range(16)]

    def partial_left(who, slot, part):
        sums = products(
            nothing,
            lambda n: right_all[who, slot, n // 8, n % 8],
            lambda n, a: gtri_float[x, part, pl.ds(a * 16 + n, 1)],
        )
        for a in range(8):
            gl_part[who, slot, part, a] = jnp.concatenate(
                [sums[a], sums[a + 8]], axis=0
            ).astype(BF16)

    def third_left(slot, part, step):
        who = (y + step) % side
        return send(
            gl_part.at[who, slot, part],
            gl_in.at[y, slot, part],
            s_gl1.at[slot, part, step - 1],
            r_gl1.at[y, slot, part],
            device(x, who, zh, zl, core),
        )

    def partials_left(phase):
        slot, part = turn_of(phase)

        def body(step, carry):
            partial_left((y + step) % side, slot, part)

            @pl.when(step < side)
            def _():
                third_left(slot, part, step).start()

            return carry

        lax.fori_loop(1, side + 1, body, 0)

    def fourth_left(slot, there):
        owner = core * half + slot
        return (
            gl_sum.at[slot, there],
            gl_own.at[zl],
            s_gl2.at[slot, there],
            r_gl2.at[zl],
            device(x, y, zh, owner, there),
            jnp.logical_and(owner == zl, there == core),
        )

    def fourth_right(slot, there):
        owner = core * half + slot
        return (
            gr_sum.at[slot, there],
            gr_own.at[zh],
            s_gr2.at[slot, there],
            r_gr2.at[zh],
            device(y, mine, zl, owner, there),
            jnp.logical_and(on_own_path, jnp.logical_and(owner == zl, there == core)),
        )

    for phase in range(side):
        partials_left(phase)

    order = sorted(range(side), key=lambda step: min(step, side - step))
    for step in order:
        who = (x + step) % side
        if step > 0:
            for there in range(2):
                arrived(gtri.at[who, there], r_gtri.at[who, there])
                widen(who, there)
        arrived(left_x.at[who], r_left_x.at[who])

        def right_block(index, carry, step=step, who=who):
            slot = index // 2
            part = index % 2
            if step == 0:
                sums = nothing
            else:
                sums = [gr_acc[index, a] for a in range(16)]
            sums = products(
                sums,
                lambda n: left_x[who, slot, n // 8, n % 8],
                lambda n, a: gtri_float[who, n // 8, pl.ds(n % 8 * 16 + part * 8 + a, 1)],
            )
            if step == order[-1]:
                for a in range(8):
                    gr_sum[slot, part, a] = jnp.concatenate(
                        [sums[a], sums[a + 8]], axis=0
                    ).astype(BF16)
                push(*fourth_right(slot, part))
            else:
                for a in range(16):
                    gr_acc[index, a] = sums[a]
            return carry

        lax.fori_loop(0, 2 * half, right_block, 0)

    def sums_left(phase):
        slot, there = turn_of(phase)
        for step in range(1, side):
            who = (y + step) % side
            arrived(gl_in.at[who, slot, there], r_gl1.at[who, slot, there])
        value = gl_part[y, slot, there].astype(F32)
        for step in range(1, side):
            value = value + gl_in[(y + step) % side, slot, there].astype(F32)
        gl_sum[slot, there] = value.astype(BF16)
        push(*fourth_left(slot, there))

    for phase in range(side):
        sums_left(phase)

    def total_of(own, sems):
        value = None
        for there in range(side):
            arrived(own.at[there], sems.at[there])
            term = own[there].astype(F32)
            value = term if value is None else value + term
        return value.reshape(128, 128)

    def project(grad, first):
        grad_proj = jnp.concatenate(
            [(grad * saved[first]).astype(BF16), (grad * saved[first + 1]).astype(BF16)], axis=-1
        )
        columns = (first - 1) * 128
        return dot_nt(grad_proj, in_weight_ref[:, columns : columns + 256])

    grad_inputs = saved[9] + project(total_of(gl_own, r_gl2), 1)
    grad_inputs = grad_inputs + project(total_of(gr_own, r_gr2), 3)
    result = saved[8] + norm_back(grad_inputs, saved[0], saved[7], norm_gain_ref[...])
    out_ref[...] = result.astype(BF16).reshape(8, 16, 128)

    @pl.when(near)
    def _():
        drain(*first_right(0))
        drain(*first_left(0))

    for there in range(1, side):
        drain(*first_right(there))
        drain(*first_left(there))
    for there in range(2):
        drain(*labels_to(there))
        drain(*logits_to(there))
    tri_copy().wait_send()
    for step in range(1, side):
        left_to(step).wait_send()
    for step in range(1, 2 * side):
        gtri_to(step).wait_send()
    for slot in range(half):
        for step in range(1, side):
            second_left(slot, step).wait_send()
            second_right(slot, step).wait_send()
        for there in range(2):
            for step in range(1, side):
                third_left(slot, there, step).wait_send()
            drain(*fourth_left(slot, there))
            drain(*fourth_right(slot, there))


def local(
    pair,
    labels,
    residue_mask,
    norm_gain,
    in_weight,
    gate_weight,
    hidden_gain,
    out_weight,
    bin_weight,
):
    side = lax.axis_size("section")
    half = side // 2
    tile = (8, 16, 128)
    sems = [
        (side,),
        (side,),
        (half, side - 1),
        (half, side - 1),
        (1,),
        (2,),
        (2,),
        (side - 1,),
        (2 * side - 1,),
        (half, 2, side - 1),
        (half, 2),
        (half, 2),
        (half, 2),
        (half, 2),
        (side, half),
        (side, half),
        (1,),
        (2,),
        (2,),
        (side,),
        (side, 2),
        (side, half, 2),
        (side,),
        (side,),
    ]
    gathered = pltpu.VMEM((side, half, 2) + tile, BF16)
    residues = residue_mask.shape[0]
    if residues < 256:
        residue_mask = jnp.pad(residue_mask, (0, 256 - residues))
    return pl.pallas_call(
        functools.partial(kernel, side),
        out_shape=jax.ShapeDtypeStruct(tile, BF16),
        in_specs=[pl.BlockSpec(memory_space=pl.ANY)] * 9,
        out_specs=pl.BlockSpec(memory_space=pltpu.VMEM),
        scratch_shapes=[
            pltpu.VMEM(tile, BF16),
            pltpu.VMEM((8, 16), jnp.int32),
            pltpu.VMEM((1, 256), jnp.int32),
            pltpu.VMEM((1, 128), F32),
            pltpu.VMEM(in_weight.shape, BF16),
            pltpu.VMEM(gate_weight.shape, BF16),
            pltpu.VMEM((1, 128), F32),
            pltpu.VMEM(out_weight.shape, BF16),
            pltpu.VMEM(bin_weight.shape[::-1], BF16),
            pltpu.SemaphoreType.DMA((9,)),
            pltpu.VMEM(tile, BF16),
            pltpu.VMEM(tile, BF16),
            gathered,
            gathered,
            pltpu.VMEM((256, 8, 128), F32),
            pltpu.VMEM((2, 128, 128), F32),
            pltpu.VMEM((128, 128), F32),
            pltpu.VMEM((2, 64, 64), BF16),
            pltpu.VMEM((2, 64, 64), BF16),
            pltpu.VMEM((8, 16), F32),
            pltpu.VMEM((2, 8, 16), F32),
            gathered,
            pltpu.VMEM((side, 2, 128, 128), BF16),
            pltpu.VMEM((side, 2, 128, 128), F32),
            gathered,
            gathered,
            pltpu.VMEM((2 * half, 16, 8, 128), F32),
            pltpu.VMEM((half, 2) + tile, BF16),
            pltpu.VMEM((half, 2) + tile, BF16),
            pltpu.VMEM((side,) + tile, BF16),
            pltpu.VMEM((side,) + tile, BF16),
            pltpu.VMEM((10, 128, 128), F32),
        ]
        + [pltpu.SemaphoreType.DMA(shape) for shape in sems],
        compiler_params=pltpu.CompilerParams(
            collective_id=0, has_side_effects=True, vmem_limit_bytes=60 * 1024 * 1024
        ),
    )(
        pair,
        labels,
        residue_mask[None, :],
        norm_gain[None, :],
        in_weight,
        gate_weight,
        hidden_gain[None, :],
        out_weight,
        bin_weight.T,
    )


def solution(mesh):
    placed = (
        P(("section", "row"), "col", None),
        P(("section", "row"), "col"),
        P(),
        P(),
        P(),
        P(),
        P(),
        P(),
        P(),
    )
    return jax.shard_map(
        local,
        mesh=mesh,
        in_specs=placed,
        out_specs=P(("section", "row"), "col", None),
        check_vma=False,
    )
```

```python
import functools

import jax
import jax.numpy as jnp
from jax import lax
from jax.experimental import pallas as pl
from jax.experimental.pallas import tpu as pltpu
from jax.sharding import PartitionSpec as P

MESH = pl.DeviceIdType.MESH
F32 = jnp.float32
BF16 = jnp.bfloat16


def norm_parts(values, gain):
    centre = values - jnp.mean(values, axis=-1, keepdims=True)
    inverse = lax.rsqrt(jnp.mean(centre * centre, axis=-1, keepdims=True) + 1e-05)
    normed = centre * inverse
    return (normed, inverse, normed * gain)


def norm_back(upstream, normed, inverse, gain):
    scaled = upstream * gain
    return inverse * (
        scaled
        - jnp.mean(scaled, axis=-1, keepdims=True)
        - normed * jnp.mean(scaled * normed, axis=-1, keepdims=True)
    )


def dot_nt(a, b):
    return lax.dot_general(a, b, (((1,), (1,)), ((), ())), preferred_element_type=F32)


def kernel(
    side,
    pair_hbm,
    labels_hbm,
    mask_hbm,
    norm_gain_hbm,
    in_weight_hbm,
    gate_weight_hbm,
    hidden_gain_hbm,
    out_weight_hbm,
    bin_weight_hbm,
    out_ref,
    pair_ref,
    labels_ref,
    mask_ref,
    norm_gain_ref,
    in_weight_ref,
    gate_weight_ref,
    hidden_gain_ref,
    out_weight_ref,
    bin_weight_ref,
    loaded,
    left_own,
    right_own,
    left_all,
    right_all,
    acc,
    tri_part,
    tri_in,
    logit_out,
    logit_in,
    label_out,
    label_in,
    left_x,
    gtri,
    gtri_float,
    gl_part,
    gl_in,
    gr_acc,
    gl_sum,
    gr_sum,
    gl_own,
    gr_own,
    saved,
    s_left1,
    s_right1,
    s_left2,
    s_right2,
    s_tri,
    s_logit,
    s_label,
    s_left_x,
    s_gtri,
    s_gl1,
    s_gl2,
    s_gr2,
    r_left1,
    r_right1,
    r_left2,
    r_right2,
    r_tri,
    r_logit,
    r_label,
    r_left_x,
    r_gtri,
    r_gl1,
    r_gl2,
    r_gr2,
):
    half = side // 2
    x = lax.axis_index("section")
    row = lax.axis_index("row")
    col = lax.axis_index("col")
    zh = row // 2
    core = row % 2
    y = col // side
    zl = col % side
    my_k_core = zl // half
    my_k_slot = zl % half
    diagonal = jnp.logical_and(x == y, zh == zl)

    def turned(a, b):
        return (2 * a + side // 2 - b + side) % side

    mine = turned(y, x)
    meet = turned(x, y)

    def device(dx, dy, dzh, dzl, dcore):
        return (dx, dzh * 2 + dcore, dy * side + dzl)

    def send(src, dst, send_sem, recv_sem, target):
        return pltpu.make_async_remote_copy(
            src_ref=src,
            dst_ref=dst,
            send_sem=send_sem,
            recv_sem=recv_sem,
            device_id=target,
            device_id_type=MESH,
        )

    def push(src, dst, send_sem, recv_sem, target, is_self):
        @pl.when(is_self)
        def _():
            pltpu.make_async_copy(src, dst, recv_sem).start()

        @pl.when(jnp.logical_not(is_self))
        def _():
            send(src, dst, send_sem, recv_sem, target).start()

    def drain(src, dst, send_sem, recv_sem, target, is_self):
        @pl.when(jnp.logical_not(is_self))
        def _():
            send(src, dst, send_sem, recv_sem, target).wait_send()

    def arrived(ref, sem):
        pltpu.make_async_copy(ref, ref, sem).wait()

    barrier = pltpu.get_barrier_semaphore()

    operands = (
        (pair_hbm, pair_ref),
        (in_weight_hbm, in_weight_ref),
        (mask_hbm, mask_ref),
        (norm_gain_hbm, norm_gain_ref),
        (labels_hbm, labels_ref),
        (gate_weight_hbm, gate_weight_ref),
        (hidden_gain_hbm, hidden_gain_ref),
        (out_weight_hbm, out_weight_ref),
        (bin_weight_hbm, bin_weight_ref),
    )

    def load(index):
        return pltpu.make_async_copy(*operands[index], loaded.at[index])

    def greet(target, is_self=None):
        def signal():
            pl.semaphore_signal(barrier, inc=1, device_id=target, device_id_type=MESH)

        if is_self is None:
            signal()
        else:
            pl.when(jnp.logical_not(is_self))(signal)

    on_own_path = jnp.logical_and(
        jnp.logical_and(x == y, meet == x), jnp.logical_and(zh == zl, core == my_k_core)
    )
    for slot in range(half):
        for there in range(2):
            source = core * half + slot
            greet(
                device(y, mine, zl, source, there),
                jnp.logical_and(on_own_path, jnp.logical_and(source == zl, there == core)),
            )
    for index in range(9):
        load(index).start()
    for slot in range(half):
        for there in range(2):
            source = core * half + slot
            greet(
                device(x, y, zh, source, there),
                jnp.logical_and(source == zl, there == core),
            )
    greet(device(x, y, zh, zl, 1 - core))
    for step in range(1, side):
        greet(device(x, (y + step) % side, zh, zl, core))
        greet(device((x + step) % side, y, zh, zl, core))
        greet(device((x + step) % side, y, zh, zl, 1 - core))
    greetings = 2 * side + 1 + 3 * (side - 1)
    awaited = (
        greetings - on_own_path.astype(jnp.int32) - (core == my_k_core).astype(jnp.int32)
    )

    load(2).wait()
    place = lax.broadcasted_iota(jnp.int32, (128, 256), 0)
    lane = lax.broadcasted_iota(jnp.int32, (128, 256), 1)
    mask_float = mask_ref[...].astype(F32)
    first_row = (x * side + zh) * 16 + core * 8
    first_col = col * 16
    mask_i = jnp.sum(
        jnp.where(lane == first_row + place // 16, mask_float, 0.0), axis=1, keepdims=True
    )
    mask_j = jnp.sum(
        jnp.where(lane == first_col + place % 16, mask_float, 0.0), axis=1, keepdims=True
    )
    pair_mask = mask_i * mask_j
    load(0).wait()
    load(3).wait()
    pair_float = pair_ref[...].astype(F32).reshape(128, 128)
    normed_in, inverse_in, scaled_in = norm_parts(pair_float, norm_gain_ref[...])
    inputs = scaled_in.astype(BF16)
    load(1).wait()

    def projected(first):
        both = jnp.dot(
            inputs, in_weight_ref[:, first : first + 256], preferred_element_type=F32
        )
        return jax.nn.sigmoid(both[:, 0:128]), both[:, 128:256]

    sig_b, value_b = projected(256)
    right_own[...] = (sig_b * value_b * pair_mask).astype(BF16).reshape(8, 16, 128)
    pl.semaphore_wait(barrier, awaited)

    def first_right(there):
        return (
            right_own,
            right_all.at[y, my_k_slot, core],
            s_right1.at[there],
            r_right1.at[my_k_slot, core],
            device(meet, x, there, zh, my_k_core),
            jnp.logical_and(on_own_path, there == zh),
        )

    def first_left(there):
        return (
            left_own,
            left_all.at[y, my_k_slot, core],
            s_left1.at[there],
            r_left1.at[my_k_slot, core],
            device(x, y, zh, there, my_k_core),
            jnp.logical_and(there == zl, core == my_k_core),
        )

    def labels_to(there):
        return (
            label_out,
            label_in.at[core],
            s_label.at[there],
            r_label.at[core],
            device(y, x, zl, zh, there),
            jnp.logical_and(diagonal, there == core),
        )

    near = zh == 0

    @pl.when(near)
    def _():
        for there in sorted(range(1, side), key=lambda there: abs(there - half)):
            push(*first_right(there))

    push(*first_right(0))

    sig_a, value_a = projected(0)
    left_own[...] = (sig_a * value_a * pair_mask).astype(BF16).reshape(8, 16, 128)
    push(*first_left(0))

    @pl.when(near)
    def _():
        for there in range(1, side):
            push(*first_left(there))

    @pl.when(jnp.logical_not(near))
    def _():
        drain(*first_left(0))
        for there in range(1, side):
            push(*first_left(there))
            push(*first_right(there))
        drain(*first_right(0))

    load(4).wait()
    label_out[...] = labels_ref[...].astype(F32)
    for index in range(5, 9):
        load(index).wait()

    saved[0] = normed_in
    saved[1] = value_a * pair_mask * sig_a * (1.0 - sig_a)
    saved[2] = sig_a * pair_mask
    saved[3] = value_b * pair_mask * sig_b * (1.0 - sig_b)
    saved[4] = sig_b * pair_mask
    saved[5] = jax.nn.sigmoid(jnp.dot(inputs, gate_weight_ref[...], preferred_element_type=F32))
    saved[6] = jnp.broadcast_to(pair_mask, (128, 128))
    saved[7] = jnp.broadcast_to(inverse_in, (128, 128))

    def second_left(slot, step):
        return send(
            left_all.at[y, slot],
            left_all.at[y, slot],
            s_left2.at[slot, step - 1],
            r_left2.at[y, slot],
            device(x, (y + step) % side, zh, zl, core),
        )

    def turn_of(phase):
        return phase // 2, phase % 2

    def second_right(slot, step):
        return send(
            right_all.at[mine, slot],
            right_all.at[mine, slot],
            s_right2.at[slot, step - 1],
            r_right2.at[mine, slot],
            device((x + step) % side, y, zh, zl, core),
        )

    for slot in range(half):
        for there in range(2):
            arrived(left_all.at[y, slot, there], r_left1.at[slot, there])
        for step in range(1, side):
            second_left(slot, step).start()

    def forward(slot):
        for part in range(2):
            arrived(right_all.at[mine, slot, part], r_right1.at[slot, part])
        for step in range(1, side):
            second_right(slot, step).start()

    acc[...] = jnp.zeros_like(acc)

    def tri_blocks(i_half, slot, j_half):
        def body(index, carry):
            i_low = index // 2 * 4
            j_low = index % 2 * 4
            base = (i_half * 8 + i_low) * 16 + j_half * 8 + j_low
            sums = [[acc[base + a * 16 + b] for b in range(4)] for a in range(4)]
            for who in range(side):
                lefts = [left_all[who, slot, i_half, i_low + a].astype(F32) for a in range(4)]
                rights = [right_all[who, slot, j_half, j_low + b].astype(F32) for b in range(4)]
                for a in range(4):
                    for b in range(4):
                        product = lefts[a] * rights[b]
                        sums[a][b] = sums[a][b] + (product[0:8] + product[8:16])
            for a in range(4):
                for b in range(4):
                    acc[base + a * 16 + b] = sums[a][b]
            return carry

        lax.fori_loop(0, 4, body, 0)

    def fold(part):
        def body(index, carry):
            at = part * 128 + index * 8
            tri_part[part, pl.ds(index * 8, 8)] = jnp.sum(acc[pl.ds(at, 8)], axis=1)
            return carry

        lax.fori_loop(0, 16, body, 0)

    def tri_copy():
        return send(
            tri_part.at[1 - core],
            tri_in,
            s_tri.at[0],
            r_tri.at[0],
            device(x, y, zh, zl, 1 - core),
        )

    forward(0)
    for phase in range(side):
        if phase % 2 == 0 and phase // 2 + 1 < half:
            forward(phase // 2 + 1)
        slot, part = turn_of(phase)
        if phase == 0:
            for step in range(1, side):
                for there in range(half):
                    who = (y + step) % side
                    arrived(left_all.at[who, there], r_left2.at[who, there])
        for step in range(1, side):
            who = (mine + step) % side
            if part == 0:
                arrived(right_all.at[who, slot], r_right2.at[who, slot])
        tri_blocks(1 - core, slot, part)
        if phase == side - 1:
            fold(1 - core)
            tri_copy().start()
        tri_blocks(core, slot, part)
    fold(core)
    arrived(tri_in, r_tri.at[0])
    for there in range(2):
        push(*labels_to(there))
    triangle = tri_part[core] + tri_in[...]

    hidden_gain = hidden_gain_ref[...]
    normed_t, inverse_t, scaled_t = norm_parts(triangle, hidden_gain)
    update = jnp.dot(scaled_t.astype(BF16), out_weight_ref[...], preferred_element_type=F32)
    gate_out = saved[5]
    pair_out = (pair_ref[...].astype(F32).reshape(128, 128) + gate_out * update).astype(BF16)
    logits = dot_nt(pair_out, bin_weight_ref[...])
    logits = logits.astype(BF16).astype(F32)
    blocks = logits.reshape(8, 2, 8, 64)
    for there in range(2):
        logit_out[there] = blocks[:, there].reshape(64, 64).astype(BF16)

    def logits_to(there):
        return (
            logit_out.at[there],
            logit_in.at[core],
            s_logit.at[there],
            r_logit.at[core],
            device(y, x, zl, zh, there),
            jnp.logical_and(diagonal, there == core),
        )

    for there in range(2):
        push(*logits_to(there))

    def left_to(step):
        who = (x + step) % side
        return send(
            left_all.at[turned(y, who)],
            left_x.at[x],
            s_left_x.at[step - 1],
            r_left_x.at[x],
            device(who, y, zh, zl, core),
        )

    for step in range(1, side):
        left_to(step).start()
    pltpu.make_async_copy(left_all.at[mine], left_x.at[x], r_left_x.at[x]).start()

    for there in range(2):
        arrived(label_in.at[there], r_label.at[there])
    place16 = lax.broadcasted_iota(jnp.int32, (128, 16), 0)
    lane16 = lax.broadcasted_iota(jnp.int32, (128, 16), 1)
    place8 = lax.broadcasted_iota(jnp.int32, (128, 8), 0)
    lane8 = lax.broadcasted_iota(jnp.int32, (128, 8), 1)
    spread = jnp.dot(
        (lane8 == place8 // 16).astype(F32), label_out[...], preferred_element_type=F32
    )
    label = jnp.sum(jnp.where(lane16 == place16 % 16, spread, 0.0), axis=1, keepdims=True)
    spread = jnp.dot(
        (lane16 == place16 % 16).astype(F32),
        label_in[...].reshape(16, 16),
        preferred_element_type=F32,
    )
    label_mirror = jnp.sum(
        jnp.where(lane16 == core * 8 + place16 // 16, spread, 0.0), axis=1, keepdims=True
    )
    bins = lax.broadcasted_iota(jnp.int32, (128, 64), 1)
    onehot = (label.astype(jnp.int32) == bins).astype(F32)
    onehot_mirror = (label_mirror.astype(jnp.int32) == bins).astype(F32)
    at_row = lax.broadcasted_iota(jnp.int32, (128, 128), 0)
    at_lane = lax.broadcasted_iota(jnp.int32, (128, 128), 1)
    turn = at_lane == (at_row // 8) % 2 * 64 + at_row % 8 * 8 + at_row // 16
    turn = turn.astype(F32).astype(BF16)
    mask_wide = saved[6]
    pair_mask = mask_wide[:, 0:64]

    for there in range(2):
        arrived(logit_in.at[there], r_logit.at[there])
    mirrored = jnp.dot(turn, logit_in[...].reshape(128, 64), preferred_element_type=F32)
    weights = jnp.exp(logits + mirrored)
    probs = weights / jnp.sum(weights, axis=-1, keepdims=True)
    grad_bins = (pair_mask * (probs - onehot)).astype(BF16).astype(F32)
    grad_mirror = (pair_mask * (probs - onehot_mirror)).astype(BF16).astype(F32)
    grad_sym = (grad_bins + grad_mirror).astype(BF16)
    grad_out = jnp.dot(grad_sym, bin_weight_ref[...], preferred_element_type=F32)
    grad_update = (grad_out * gate_out).astype(BF16)
    grad_scaled = dot_nt(grad_update, out_weight_ref[...])
    grad_triangle = norm_back(grad_scaled, normed_t, inverse_t, hidden_gain)
    gtri[x, core] = grad_triangle.astype(BF16)

    def gtri_to(step):
        other = (x * 2 + core + step) % (2 * side)
        return send(
            gtri.at[x, core],
            gtri.at[x, core],
            s_gtri.at[step - 1],
            r_gtri.at[x, core],
            device(other // 2, y, zh, zl, other % 2),
        )

    for step in range(1, 2 * side):
        gtri_to(step).start()
    grad_gate = (grad_out * update * gate_out * (1.0 - gate_out)).astype(BF16)
    saved[8] = grad_out
    saved[9] = dot_nt(grad_gate, gate_weight_ref[...])

    def widen(who, part):
        gtri_float[who, part] = gtri[who, part].astype(F32)

    widen(x, core)
    arrived(gtri.at[x, 1 - core], r_gtri.at[x, 1 - core])
    widen(x, 1 - core)

    def products(sums, tile_of, factor_of):
        low, high = list(sums[0:8]), list(sums[8:16])
        for n in range(16):
            tile = tile_of(n).astype(F32)
            for a in range(8):
                factor = jnp.broadcast_to(factor_of(n, a), (8, 128))
                low[a] = low[a] + factor * tile[0:8]
                high[a] = high[a] + factor * tile[8:16]
        return low + high

    nothing = [jnp.zeros((8, 128), F32) for _ in range(16)]

    def partial_left(who, slot, part):
        sums = products(
            nothing,
            lambda n: right_all[who, slot, n // 8, n % 8],
            lambda n, a: gtri_float[x, part, pl.ds(a * 16 + n, 1)],
        )
        for a in range(8):
            gl_part[who, slot, part, a] = jnp.concatenate(
                [sums[a], sums[a + 8]], axis=0
            ).astype(BF16)

    def third_left(slot, part, step):
        who = (y + step) % side
        return send(
            gl_part.at[who, slot, part],
            gl_in.at[y, slot, part],
            s_gl1.at[slot, part, step - 1],
            r_gl1.at[y, slot, part],
            device(x, who, zh, zl, core),
        )

    def partials_left(phase):
        slot, part = turn_of(phase)

        def body(step, carry):
            partial_left((y + step) % side, slot, part)

            @pl.when(step < side)
            def _():
                third_left(slot, part, step).start()

            return carry

        lax.fori_loop(1, side + 1, body, 0)

    def fourth_left(slot, there):
        owner = core * half + slot
        return (
            gl_sum.at[slot, there],
            gl_own.at[zl],
            s_gl2.at[slot, there],
            r_gl2.at[zl],
            device(x, y, zh, owner, there),
            jnp.logical_and(owner == zl, there == core),
        )

    def fourth_right(slot, there):
        owner = core * half + slot
        return (
            gr_sum.at[slot, there],
            gr_own.at[zh],
            s_gr2.at[slot, there],
            r_gr2.at[zh],
            device(y, mine, zl, owner, there),
            jnp.logical_and(on_own_path, jnp.logical_and(owner == zl, there == core)),
        )

    for phase in range(side):
        partials_left(phase)

    order = sorted(range(side), key=lambda step: min(step, side - step))
    for step in order:
        who = (x + step) % side
        if step > 0:
            for there in range(2):
                arrived(gtri.at[who, there], r_gtri.at[who, there])
                widen(who, there)
        arrived(left_x.at[who], r_left_x.at[who])

        def right_block(index, carry, step=step, who=who):
            slot = index // 2
            part = index % 2
            if step == 0:
                sums = nothing
            else:
                sums = [gr_acc[index, a] for a in range(16)]
            sums = products(
                sums,
                lambda n: left_x[who, slot, n // 8, n % 8],
                lambda n, a: gtri_float[who, n // 8, pl.ds(n % 8 * 16 + part * 8 + a, 1)],
            )
            if step == order[-1]:
                for a in range(8):
                    gr_sum[slot, part, a] = jnp.concatenate(
                        [sums[a], sums[a + 8]], axis=0
                    ).astype(BF16)
                push(*fourth_right(slot, part))
            else:
                for a in range(16):
                    gr_acc[index, a] = sums[a]
            return carry

        lax.fori_loop(0, 2 * half, right_block, 0)

    def sums_left(phase):
        slot, there = turn_of(phase)
        for step in range(1, side):
            who = (y + step) % side
            arrived(gl_in.at[who, slot, there], r_gl1.at[who, slot, there])
        value = gl_part[y, slot, there].astype(F32)
        for step in range(1, side):
            value = value + gl_in[(y + step) % side, slot, there].astype(F32)
        gl_sum[slot, there] = value.astype(BF16)
        push(*fourth_left(slot, there))

    for phase in range(side):
        sums_left(phase)

    def total_of(own, sems):
        value = None
        for there in range(side):
            arrived(own.at[there], sems.at[there])
            term = own[there].astype(F32)
            value = term if value is None else value + term
        return value.reshape(128, 128)

    def project(grad, first):
        grad_proj = jnp.concatenate(
            [(grad * saved[first]).astype(BF16), (grad * saved[first + 1]).astype(BF16)], axis=-1
        )
        columns = (first - 1) * 128
        return dot_nt(grad_proj, in_weight_ref[:, columns : columns + 256])

    grad_inputs = saved[9] + project(total_of(gl_own, r_gl2), 1)
    grad_inputs = grad_inputs + project(total_of(gr_own, r_gr2), 3)
    result = saved[8] + norm_back(grad_inputs, saved[0], saved[7], norm_gain_ref[...])
    out_ref[...] = result.astype(BF16).reshape(8, 16, 128)

    @pl.when(near)
    def _():
        drain(*first_right(0))
        drain(*first_left(0))

    for there in range(1, side):
        drain(*first_right(there))
        drain(*first_left(there))
    for there in range(2):
        drain(*labels_to(there))
        drain(*logits_to(there))
    tri_copy().wait_send()
    for step in range(1, side):
        left_to(step).wait_send()
    for step in range(1, 2 * side):
        gtri_to(step).wait_send()
    for slot in range(half):
        for step in range(1, side):
            second_left(slot, step).wait_send()
            second_right(slot, step).wait_send()
        for there in range(2):
            for step in range(1, side):
                third_left(slot, there, step).wait_send()
            drain(*fourth_left(slot, there))
            drain(*fourth_right(slot, there))


def local(
    pair,
    labels,
    residue_mask,
    norm_gain,
    in_weight,
    gate_weight,
    hidden_gain,
    out_weight,
    bin_weight,
):
    side = lax.axis_size("section")
    half = side // 2
    tile = (8, 16, 128)
    sems = [
        (side,),
        (side,),
        (half, side - 1),
        (half, side - 1),
        (1,),
        (2,),
        (2,),
        (side - 1,),
        (2 * side - 1,),
        (half, 2, side - 1),
        (half, 2),
        (half, 2),
        (half, 2),
        (half, 2),
        (side, half),
        (side, half),
        (1,),
        (2,),
        (2,),
        (side,),
        (side, 2),
        (side, half, 2),
        (side,),
        (side,),
    ]
    gathered = pltpu.VMEM((side, half, 2) + tile, BF16)
    residues = residue_mask.shape[0]
    if residues < 256:
        residue_mask = jnp.pad(residue_mask, (0, 256 - residues))
    return pl.pallas_call(
        functools.partial(kernel, side),
        out_shape=jax.ShapeDtypeStruct(tile, BF16),
        in_specs=[pl.BlockSpec(memory_space=pl.ANY)] * 9,
        out_specs=pl.BlockSpec(memory_space=pltpu.VMEM),
        scratch_shapes=[
            pltpu.VMEM(tile, BF16),
            pltpu.VMEM((8, 16), jnp.int32),
            pltpu.VMEM((1, 256), jnp.int32),
            pltpu.VMEM((1, 128), F32),
            pltpu.VMEM(in_weight.shape, BF16),
            pltpu.VMEM(gate_weight.shape, BF16),
            pltpu.VMEM((1, 128), F32),
            pltpu.VMEM(out_weight.shape, BF16),
            pltpu.VMEM(bin_weight.shape[::-1], BF16),
            pltpu.SemaphoreType.DMA((9,)),
            pltpu.VMEM(tile, BF16),
            pltpu.VMEM(tile, BF16),
            gathered,
            gathered,
            pltpu.VMEM((256, 8, 128), F32),
            pltpu.VMEM((2, 128, 128), F32),
            pltpu.VMEM((128, 128), F32),
            pltpu.VMEM((2, 64, 64), BF16),
            pltpu.VMEM((2, 64, 64), BF16),
            pltpu.VMEM((8, 16), F32),
            pltpu.VMEM((2, 8, 16), F32),
            gathered,
            pltpu.VMEM((side, 2, 128, 128), BF16),
            pltpu.VMEM((side, 2, 128, 128), F32),
            gathered,
            gathered,
            pltpu.VMEM((2 * half, 16, 8, 128), F32),
            pltpu.VMEM((half, 2) + tile, BF16),
            pltpu.VMEM((half, 2) + tile, BF16),
            pltpu.VMEM((side,) + tile, BF16),
            pltpu.VMEM((side,) + tile, BF16),
            pltpu.VMEM((10, 128, 128), F32),
        ]
        + [pltpu.SemaphoreType.DMA(shape) for shape in sems],
        compiler_params=pltpu.CompilerParams(
            collective_id=0, has_side_effects=True, vmem_limit_bytes=60 * 1024 * 1024
        ),
    )(
        pair,
        labels,
        residue_mask[None, :],
        norm_gain[None, :],
        in_weight,
        gate_weight,
        hidden_gain[None, :],
        out_weight,
        bin_weight.T,
    )


def solution(mesh):
    placed = (
        P(("section", "row"), "col", None),
        P(("section", "row"), "col"),
        P(),
        P(),
        P(),
        P(),
        P(),
        P(),
        P(),
    )
    return jax.shard_map(
        local,
        mesh=mesh,
        in_specs=placed,
        out_specs=P(("section", "row"), "col", None),
        check_vma=False,
    )
```
